256 devices in a mesh: dp: 32 (over x, y, core), tensor: 8 (over z).
Axes of the slice: x: 4, y: 4, z: 8, core: 2. Of those that a mesh axis runs over, the one named last changes fastest.
Arguments:
- residual_in: bfloat16 [4096, 7168], P('dp', 'tensor'), may hold values from -6 to 6
- queries: bfloat16 [4096, 64, 192], P('dp', 'tensor'), may hold values from -41 to 41
- latent: bfloat16 [4096, 576], P('dp'), may hold values from -6 to 6
- latent_up: bfloat16 [64, 512, 256], P('tensor'), may hold values from -0.25 to 0.25
- out_proj: bfloat16 [8192, 7168], P('tensor', 'dp'), may hold values from -0.0625 to 0.0625
- norm_gain: bfloat16 [7168], P('tensor'), may hold values from 0.099609375 to 1.8984375
- expert_ids: int32 [4096, 8], P('dp'), may hold values from 0 to 255, all different within a row; in each aligned block of 128 rows (0 to 127, 128 to 255, ...) at most 8 rows name the same one
- gate_num: int32 [4096, 8], P('dp'), may hold values from 16 to 256
- slot_table: int32 [256], replicated, may hold values from 0 to 255, each once
- gate_proj: bfloat16 [32, 7168, 1024], P('dp', 'tensor'), may hold values from -0.0625 to 0.0625
- up_proj: bfloat16 [32, 7168, 1024], P('dp', 'tensor'), may hold values from -0.0625 to 0.0625
- down_proj: bfloat16 [32, 1024, 7168], P('dp', 'tensor'), may hold values from -0.1875 to 0.1875
- inv_chol: float32 [32, 1024, 128], P('dp', 'tensor'), as said below
Outputs:
- residual_out: bfloat16 [4096, 7168], P('dp', 'tensor')
- moe_out: bfloat16 [4096, 7168], P('dp', 'tensor')
- down_quant: bfloat16 [32, 1024, 7168], P('dp', 'tensor')
- panel_gram: float32 [32, 1024, 128], P('dp', 'tensor')
The draws below stay inside these ranges and needn't reach their ends.
Inputs may be any that keep to these rules, and one draw needn't show every extreme that they name: `expert_ids`: in the rows of one sequence of 128 tokens no expert is named by more than 8 rows; a row names 8 different experts. `slot_table`: each number of 0 to 255 appears once. `inv_chol`: each 128 x 128 block along the second dimension is upper triangular with a positive diagonal of at least one half.
All inputs are finite; a program needn't handle non-finite values.
Results may differ from the reference program's by a relative error of at most 0.039.
Values may be sent and summed in bfloat16 or wider, within the bound.
A program may use at most 192 MiB of HBM per device.

```python
import math
import jax
import jax.numpy as jnp
import numpy as np
from jax import lax

D = 7168
FF = 1024
HEADS = 64
NOPE = 128
ROPE = 64
VHEAD = 128
LATENT = 512
EXPERTS_ALL = 256
TOPK = 8
PANEL = 128
BLK = 16
TOK_DEV = 128
KEPT = 32
CAP = 8
TOKENS = 4096
UNITS = 128
HEADS_DEV = 8
N_DP = 32
N_TENSOR = 8


def draw_queries(key, part):
    key = jax.random.fold_in(key, 11)
    shape = (TOKENS, HEADS, NOPE + ROPE)
    base = jnp.clip(jax.random.normal(jax.random.fold_in(key, 1), shape, jnp.float32), -4.0, 4.0)
    return base.astype(jnp.bfloat16)


def draw_inv_chol(key, part):
    key = jax.random.fold_in(key, 23)
    blocks = KEPT * FF // PANEL
    diagonal = jnp.exp(jax.random.uniform(jax.random.fold_in(key, 1), (blocks, PANEL), jnp.float32, math.log(0.5), math.log(1.5)))
    spread = jax.random.normal(jax.random.fold_in(key, 2), (blocks, PANEL, PANEL), jnp.float32) * (3.5 / math.sqrt(PANEL))
    upper = jnp.triu(spread, 1) + diagonal[:, :, None] * jnp.eye(PANEL, dtype=jnp.float32)[None]
    return upper.reshape(KEPT, FF, PANEL)


def set_ends(entries, key, least, top_value):
    longest = entries.shape.index(max(entries.shape))
    spots = []
    for shift in (0, 1):
        where = [jax.random.randint(jax.random.fold_in(key, axis), (), 0, length) for axis, length in enumerate(entries.shape)]
        where[longest] = (where[longest] + shift) % entries.shape[longest]
        spots.append(tuple(where))
    return entries.at[spots[0]].set(least).at[spots[1]].set(top_value)


def level_of(key, shape, cuts, least, largest):
    def one(dim, shards_of):
        heights = jax.random.uniform(jax.random.fold_in(jax.random.fold_in(key, 6), dim), (shards_of,), jnp.float32, least / len(cuts), largest / len(cuts))
        return jnp.repeat(jnp.exp(heights), shape[dim] // shards_of).reshape((-1,) + (1,) * (len(shape) - dim - 1))

    factor_of = one(*cuts[0])
    for cut in cuts[1:]:
        factor_of = factor_of * one(*cut)
    return factor_of


def routed_block(rng, own, number, rows, amount, top, most, slope):
    order = jax.random.permutation(rng, amount)
    crowded, usual = shares(amount, rows * top, most, slope, True), shares(amount, rows * top, most, slope, False)
    places = jnp.arange(amount)

    def named(tallies, rotation):
        used = int((tallies > 0).sum())
        fixed = max(1, used // 4)
        moved = fixed + (places - fixed + rotation * (used - fixed)) % max(1, amount - fixed)
        return jnp.zeros((amount,), jnp.int32).at[order[jnp.where(places < fixed, places, moved)]].set(jnp.asarray(tallies, jnp.int32))

    tallies = jnp.where(number % 4 == 0, named(crowded, number // 4), named(usual, number - number // 4 - 1))
    mixed = jax.random.permutation(jax.random.fold_in(own, 3), amount)
    donor, sink = mixed[0:amount // 2 * 2:2], mixed[1:amount // 2 * 2:2]
    slack = jnp.minimum(tallies[donor] - 1, most - tallies[sink]) // 2
    slack = jnp.where((donor == order[0]) | (sink == order[0]) | (tallies[sink] == 0), 0, jnp.maximum(slack, 0))
    moved = jax.random.randint(jax.random.fold_in(own, 4), (amount // 2,), 0, 1 << 20) % (slack + 1)
    tallies = tallies.at[donor].add(-moved).at[sink].add(moved)
    items = jnp.searchsorted(jnp.cumsum(tallies), jnp.arange(rows * top), side="right").astype(jnp.int32)
    table = items.reshape(top, rows).T
    table = table[jax.random.permutation(jax.random.fold_in(own, 1), rows)]
    rotation = jax.random.randint(jax.random.fold_in(own, 2), (rows, 1), 0, top)
    return jnp.take_along_axis(table, (jnp.arange(top)[None, :] + rotation) % top, axis=1)


def shares(number_of, total, limit, slope, full):
    loads = [(1 << 20) // math.isqrt(rank ** slope) + 1 for rank in range(1, number_of + 1)]
    largest = limit if full else min(limit, max(-(-total // number_of), total * loads[0] // sum(loads)))
    least = 1 if total - largest >= number_of - 1 else 0
    counts, rest = [largest] + [least] * (number_of - 1), total - largest - least * (number_of - 1)
    while rest > 0:
        candidates = [i for i in range(1, number_of) if counts[i] < largest] or [i for i in range(1, number_of) if counts[i] < limit]
        whole, left = sum([loads[i] for i in candidates]), rest
        for i in candidates:
            more = min(limit - counts[i], max(1, left * loads[i] // whole), rest)
            counts[i] = counts[i] + more
            rest = rest - more
    return np.array(counts)


def centred(own_key, extent, scale, limit, pieces=(), kind=jnp.bfloat16):
    loudness = level_of(own_key, extent, pieces, -0.22, 0.18) if pieces else 1.0
    entries = jax.random.normal(own_key, extent, jnp.float32) * scale * loudness
    return jnp.minimum(jnp.maximum(entries, -limit), limit).astype(kind)


def setup_inputs(seed: int = 0) -> dict:
    key_list = jax.random.split(jax.random.key(seed), 14)
    residual_in = centred(key_list[0], (TOKENS, D), 1.0, 6.0, ((0, 32), (1, 8)))
    queries = draw_queries(jax.random.fold_in(key_list[13], 71), 0)
    latent = centred(key_list[2], (TOKENS, LATENT + ROPE), 1.0, 6.0, ((0, 32),))
    latent_up = centred(key_list[3], (HEADS, LATENT, NOPE + VHEAD), LATENT ** -0.5, 0.25, ((0, 8),))
    out_proj = centred(key_list[4], (HEADS * VHEAD, D), (HEADS * VHEAD) ** -0.5, 0.0625, ((0, 8), (1, 32)))
    norm_gain = jnp.clip(1.0 + 0.18 * jax.random.normal(key_list[5], (D,), jnp.float32), 0.099609375, 1.8984375).astype(jnp.bfloat16)
    expert_ids_keys = jax.random.split(jax.random.fold_in(key_list[6], 1), TOKENS // TOK_DEV)
    expert_ids_turns = jax.random.permutation(jax.random.fold_in(key_list[6], 3), TOKENS // TOK_DEV)
    expert_ids = jax.vmap(lambda own, number: routed_block(jax.random.fold_in(key_list[6], 2), own, number, TOK_DEV, EXPERTS_ALL, TOPK, CAP, 2))(expert_ids_keys, expert_ids_turns).reshape((TOKENS, TOPK))
    gate_num = set_ends(jax.random.randint(key_list[7], (TOKENS, TOPK), 16, 257), jax.random.fold_in(key_list[7], 1), 16, 256).astype(jnp.int32)
    slot_table = jax.random.permutation(key_list[8], EXPERTS_ALL).astype(jnp.int32)
    gate_proj = centred(key_list[9], (KEPT, D, FF), D ** -0.5, 0.0625, ((0, 32), (1, 8)))
    up_proj = centred(key_list[10], (KEPT, D, FF), D ** -0.5, 0.0625, ((0, 32), (1, 8)))
    down_proj = centred(key_list[11], (KEPT, FF, D), FF ** -0.5, 0.1875, ((0, 32), (1, 8)))
    inv_chol = draw_inv_chol(jax.random.fold_in(key_list[13], 71), 0)
    return {"residual_in": residual_in, "queries": queries, "latent": latent, "latent_up": latent_up, "out_proj": out_proj, "norm_gain": norm_gain, "expert_ids": expert_ids, "gate_num": gate_num, "slot_table": slot_table, "gate_proj": gate_proj, "up_proj": up_proj, "down_proj": down_proj, "inv_chol": inv_chol}


def soft_levels(values, low, step):
    scaled = jnp.clip((values - low) / step, 0.0, 15.0)
    return low + step * (scaled - jnp.sin(2.0 * math.pi * scaled) / (2.0 * math.pi))

def quantize_panel(weight, upper):
    low = lax.optimization_barrier(jnp.min(weight, axis=0))
    high = lax.optimization_barrier(jnp.max(weight, axis=0))
    step = (high - low) / 15.0 + 1e-05
    strict = jnp.triu(upper, 1)
    diagonal = jnp.diagonal(upper)
    remaining = weight
    finished = []
    for begin in range(0, weight.shape[0], BLK):
        current = [remaining[offset] for offset in range(BLK)]
        remaining = remaining[BLK:]
        errors = []
        for offset in range(BLK):
            column = begin + offset
            levels = soft_levels(current[offset], low, step)
            finished.append(levels)
            error = (current[offset] - levels) / diagonal[column]
            errors.append(error)
            for later in range(offset + 1, BLK):
                current[later] = current[later] - strict[column, begin + later] * error
        if remaining.shape[0] > 0:
            coupling = strict[begin:begin + BLK, begin + BLK:]
            remaining = remaining - jnp.dot(coupling.T, jnp.stack(errors), precision=lax.Precision.HIGHEST)
    return jnp.stack(finished)

def reference(residual_in, queries, latent, latent_up, out_proj, norm_gain, expert_ids, gate_num, slot_table, gate_proj, up_proj, down_proj, inv_chol):
    scale = 1.0 / math.sqrt(NOPE + ROPE)
    query_seq = queries.reshape(N_DP, TOK_DEV, HEADS, NOPE + ROPE)
    latent_seq = latent.reshape(N_DP, TOK_DEV, LATENT + ROPE)
    causal = jnp.arange(TOK_DEV)[None, :] <= jnp.arange(TOK_DEV)[:, None]

    def attend(pair):
        query_blk, latent_blk = pair
        key_value = jnp.einsum('tc,hcd->thd', latent_blk[:, :LATENT].astype(jnp.float32), latent_up.astype(jnp.float32)).astype(jnp.bfloat16)
        rotary = jnp.broadcast_to(latent_blk[:, None, LATENT:], (TOK_DEV, HEADS, ROPE))
        keys = jnp.concatenate([key_value[:, :, :NOPE], rotary], axis=2)
        scores = jnp.einsum('thd,shd->hts', query_blk.astype(jnp.float32), keys.astype(jnp.float32)) * scale
        scores = jnp.where(causal[None], scores, -1e+30)
        top = lax.optimization_barrier(jnp.max(scores, axis=2, keepdims=True))
        expo = jnp.exp(scores - top)
        probs = (expo / lax.optimization_barrier(jnp.sum(expo, axis=2, keepdims=True))).astype(jnp.bfloat16)
        values = key_value[:, :, NOPE:]
        result = jnp.einsum('hts,shd->thd', probs.astype(jnp.float32), values.astype(jnp.float32)).astype(jnp.bfloat16)
        return result.reshape(TOK_DEV, HEADS * VHEAD)
    attended = lax.map(attend, (query_seq, latent_seq)).reshape(TOKENS, HEADS * VHEAD)
    group_cols = HEADS_DEV * VHEAD
    attn = jnp.zeros((TOKENS, D), jnp.float32)
    for group in range(N_TENSOR):
        piece = jnp.dot(attended[:, group * group_cols:(group + 1) * group_cols], out_proj[group * group_cols:(group + 1) * group_cols], preferred_element_type=jnp.float32)
        attn = attn + lax.optimization_barrier(piece.astype(jnp.bfloat16)).astype(jnp.float32)
    residual_out = (residual_in.astype(jnp.float32) + attn).astype(jnp.bfloat16)
    wide = residual_out.astype(jnp.float32)
    normed = (wide * lax.rsqrt(lax.optimization_barrier(jnp.mean(wide * wide, axis=1, keepdims=True)) + 1e-06) * norm_gain.astype(jnp.float32)).astype(jnp.bfloat16)
    slots = slot_table[expert_ids]
    kept = slots < KEPT
    onehot = (slots[:, :, None] == jnp.arange(KEPT, dtype=jnp.int32)[None, None, :]).astype(jnp.int32)
    onehot_seq = onehot.reshape(N_DP, TOK_DEV * TOPK, KEPT)
    before = jnp.cumsum(onehot_seq, axis=1) - onehot_seq
    position = lax.optimization_barrier(jnp.sum(before * onehot_seq, axis=2)).reshape(TOKENS, TOPK).astype(jnp.int32)
    sequence = jnp.broadcast_to((jnp.arange(TOKENS, dtype=jnp.int32) // TOK_DEV)[:, None], (TOKENS, TOPK))
    token_index = jnp.broadcast_to(jnp.arange(TOKENS, dtype=jnp.int32)[:, None], (TOKENS, TOPK))
    safe_slot = jnp.where(kept, slots, KEPT).astype(jnp.int32)
    table = jnp.full((KEPT, N_DP, CAP), TOKENS, jnp.int32)
    table = table.at[safe_slot, sequence, position].set(token_index, mode='drop')
    padded = jnp.concatenate([normed, jnp.zeros((1, D), jnp.bfloat16)], axis=0)
    slot_rows = N_DP * CAP
    panels_per = FF // PANEL

    def expert(pack):
        index_tab, gate_w, up_w, down_w, upper_w = pack
        inputs = padded[index_tab.reshape(-1)]
        gate = jnp.dot(inputs, gate_w, preferred_element_type=jnp.float32)
        upval = jnp.dot(inputs, up_w, preferred_element_type=jnp.float32)
        hidden = (jax.nn.silu(gate) * upval).astype(jnp.bfloat16)
        split = hidden.reshape(slot_rows, panels_per, PANEL).astype(jnp.float32)
        gram = (jnp.einsum('rpi,rpj->pij', split, split) / slot_rows).reshape(FF, PANEL)
        panels = down_w.astype(jnp.float32).reshape(panels_per, PANEL, D)
        uppers = upper_w.reshape(panels_per, PANEL, PANEL)
        quant = jax.vmap(quantize_panel)(panels, uppers).reshape(FF, D).astype(jnp.bfloat16)
        total = jnp.zeros((slot_rows, D), jnp.float32)
        for group in range(N_TENSOR):
            piece = jnp.dot(hidden[:, group * UNITS:(group + 1) * UNITS], quant[group * UNITS:(group + 1) * UNITS], preferred_element_type=jnp.float32)
            total = total + lax.optimization_barrier(piece.astype(jnp.bfloat16)).astype(jnp.float32)
        return (total.astype(jnp.bfloat16).reshape(N_DP, CAP, D), quant, gram)
    expert_rows, down_quant, panel_gram = lax.map(expert, (table, gate_proj, up_proj, down_proj, inv_chol))
    moe = jnp.zeros((TOKENS, D), jnp.float32)
    clipped = jnp.minimum(slots, KEPT - 1).astype(jnp.int32)
    safe_pos = jnp.minimum(position, CAP - 1).astype(jnp.int32)
    for pick in range(TOPK):
        weight = jnp.where(kept[:, pick], gate_num[:, pick].astype(jnp.float32) / 256.0, 0.0)
        values = expert_rows[clipped[:, pick], sequence[:, pick], safe_pos[:, pick]].astype(jnp.float32)
        moe = moe + weight[:, None] * values
    return (residual_out, moe.astype(jnp.bfloat16), down_quant, panel_gram)
```

```python
import math

import jax
import jax.numpy as jnp
import numpy as np
from jax import lax
from jax.experimental import pallas as pl
from jax.experimental.pallas import tpu as pltpu
from jax.sharding import PartitionSpec as P

D = 7168
NOPE = 128
ROPE = 64
VHEAD = 128
LATENT = 512
PANEL = 128
BLK = 16
CAP = 8
NSUB = 8
LANES = 128
F32 = jnp.float32
BF16 = jnp.bfloat16


def _sin_coeffs():
    n = 400
    u = (0.5 * np.cos(np.pi * (np.arange(n) + 0.5) / (2 * n))) ** 2
    r = np.sqrt(u)
    target = np.sin(2 * np.pi * r) / (2 * np.pi * r)
    vand = np.vander(u, 8, increasing=True)
    return [float(c) for c in np.linalg.lstsq(vand * r[:, None], target * r, rcond=None)[0]]

SINC = _sin_coeffs()

def quant_kernel(us_ref, w_ref, u_ref, sel_ref, q_ref, wnat, cur, err, qi, lo, st, rs):
    tiles = w_ref.shape[1] // (NSUB * LANES)
    width = tiles * LANES
    for c in range(NSUB):
        cols = slice(c * width, (c + 1) * width)
        chunk = w_ref[:, cols].astype(F32)
        wnat[:, cols] = chunk
        low = jnp.min(chunk, axis=0, keepdims=True)
        high = jnp.max(chunk, axis=0, keepdims=True)
        step = (high - low) / 15.0 + 1e-05
        inverse = 1.0 / step
        for j in range(tiles):
            lanes = slice(j * LANES, (j + 1) * LANES)
            lo[j, c:c + 1, :] = low[:, lanes]
            st[j, c:c + 1, :] = step[:, lanes]
            rs[j, c:c + 1, :] = inverse[:, lanes]

    def block(b, first):
        base = pl.multiple_of(b * BLK, BLK)
        for c in range(NSUB):
            for j in range(tiles):
                at = c * width + j * LANES
                cur[j, pl.ds(c, BLK, NSUB), :] = wnat[pl.ds(base, BLK), at:at + LANES]
        low, step, rstep = lo[...], st[...], rs[...]
        for i in range(BLK):
            rows = slice(i * NSUB, (i + 1) * NSUB)
            x = cur[:, rows, :]
            for k in range(i):
                x = x - us_ref[base + k, base + i] * err[:, k * NSUB:(k + 1) * NSUB, :]
            inv = 1.0 / jnp.full((NSUB, LANES), us_ref[base + i, base + i], F32)
            t = jnp.minimum(jnp.maximum((x - low) * rstep, 0.0), 15.0)
            r = t - jnp.floor(t + 0.5)
            v = r * r
            v2 = v * v
            poly = (SINC[0] + SINC[1] * v) + (SINC[2] + SINC[3] * v) * v2
            poly = poly + ((SINC[4] + SINC[5] * v) + (SINC[6] + SINC[7] * v) * v2) * (v2 * v2)
            level = low + step * (t - r * poly)
            err[:, rows, :] = (x - level) * inv[None]
            qi[:, rows, :] = level
        if first is not None:
            parts = jnp.concatenate(split3(u_ref[pl.ds(base, BLK), :]), axis=0)
            coupling = lax.dot_general(
                parts, sel_ref[...], (((0,), (0,)), ((), ())), preferred_element_type=F32
            ).astype(BF16)[first:, :]
        for c in range(NSUB):
            cols = slice(c * width, (c + 1) * width)
            spread = [qi[j, pl.ds(c, BLK, NSUB), :] for j in range(tiles)]
            q_ref[pl.ds(base, BLK), cols] = jnp.concatenate(spread, axis=1).astype(BF16)
            if first is not None:
                spread = [err[j, pl.ds(c, BLK, NSUB), :] for j in range(tiles)]
                e = split3(jnp.concatenate(spread, axis=1))
                stacked = jnp.concatenate([e[p] for p in PART_E], axis=0)
                wnat[first:, cols] = wnat[first:, cols] - jnp.dot(
                    coupling, stacked, preferred_element_type=F32
                )

    def early(b, carry):
        block(b, BLK)
        return carry

    def late(b, carry):
        block(b, 5 * BLK)
        return carry

    lax.fori_loop(0, 4, early, 0)
    lax.fori_loop(4, 7, late, 0)
    block(7, None)


PART_U = (0, 0, 0, 1, 1, 2, 1, 2)
PART_E = (0, 1, 2, 0, 1, 0, 2, 1)

def split3(a):
    a1 = a.astype(BF16)
    rest = a - a1.astype(F32)
    a2 = rest.astype(BF16)
    return a1, a2, (rest - a2.astype(F32)).astype(BF16)


def selector():
    sel = np.zeros((3 * BLK, 8 * BLK), np.float32)
    for slot, part in enumerate(PART_U):
        for i in range(BLK):
            sel[part * BLK + i, slot * BLK + i] = 1
    return sel


def quantize(weight, upper):
    width = weight.shape[1]
    tiles = width // (NSUB * LANES)
    vmem = pl.BlockSpec(memory_space=pltpu.VMEM)
    return pl.pallas_call(
        quant_kernel,
        out_shape=jax.ShapeDtypeStruct((PANEL, width), BF16),
        in_specs=[pl.BlockSpec(memory_space=pltpu.SMEM), vmem, vmem, vmem],
        out_specs=vmem,
        scratch_shapes=[
            pltpu.VMEM((PANEL, width), F32),
            pltpu.VMEM((tiles, BLK * NSUB, LANES), F32),
            pltpu.VMEM((tiles, BLK * NSUB, LANES), F32),
            pltpu.VMEM((tiles, BLK * NSUB, LANES), F32),
            pltpu.VMEM((tiles, NSUB, LANES), F32),
            pltpu.VMEM((tiles, NSUB, LANES), F32),
            pltpu.VMEM((tiles, NSUB, LANES), F32),
        ],
        compiler_params=pltpu.CompilerParams(vmem_limit_bytes=48 * 2**20),
    )(upper, weight, upper, jnp.asarray(selector(), BF16))


def shards(
    residual_in,
    queries,
    latent,
    latent_up,
    out_proj,
    norm_gain,
    expert_ids,
    gate_num,
    slot_table,
    gate_proj,
    up_proj,
    down_proj,
    inv_chol,
):
    seq_len = queries.shape[0]
    head_count = queries.shape[1]
    scale = 1.0 / math.sqrt(NOPE + ROPE)
    key_value = jnp.einsum(
        "tc,hcd->thd", latent[:, :LATENT], latent_up, preferred_element_type=jnp.float32
    ).astype(jnp.bfloat16)
    rotary = jnp.broadcast_to(latent[:, None, LATENT:], (seq_len, head_count, ROPE))
    keys = jnp.concatenate([key_value[:, :, :NOPE], rotary], axis=2)
    scores = jnp.einsum("thd,shd->hts", queries, keys, preferred_element_type=jnp.float32) * scale
    causal = jnp.arange(seq_len)[None, :] <= jnp.arange(seq_len)[:, None]
    scores = jnp.where(causal[None], scores, -1e30)
    top = jnp.max(scores, axis=2, keepdims=True)
    expo = jnp.exp(scores - top)
    probs = (expo / jnp.sum(expo, axis=2, keepdims=True)).astype(jnp.bfloat16)
    result = jnp.einsum(
        "hts,shd->thd", probs, key_value[:, :, NOPE:], preferred_element_type=jnp.float32
    )
    attended = result.astype(jnp.bfloat16).reshape(seq_len, head_count * VHEAD)
    partial_out = jnp.dot(
        attended,
        lax.all_gather(out_proj, "dp", axis=1, tiled=True),
        preferred_element_type=jnp.float32,
    )
    attn = lax.psum_scatter(
        partial_out.astype(jnp.bfloat16), "tensor", scatter_dimension=1, tiled=True
    ).astype(jnp.float32)
    residual_out = (residual_in.astype(jnp.float32) + attn).astype(jnp.bfloat16)
    wide = residual_out.astype(jnp.float32)
    square_tot = lax.psum(jnp.sum(wide * wide, axis=1), "tensor")
    normed = (
        wide * lax.rsqrt(square_tot / D + 1e-06)[:, None] * norm_gain.astype(jnp.float32)
    ).astype(jnp.bfloat16)
    owners = lax.axis_size("dp")
    capacity = CAP
    experts_all = slot_table.shape[0]
    named = expert_ids[:, :, None] == jnp.arange(experts_all, dtype=jnp.int32)[None, None, :]
    picks = jnp.sum(named.astype(F32), axis=1).astype(BF16)
    gates = jnp.sum(jnp.where(named, gate_num[:, :, None], 0), axis=1).astype(BF16)
    kept = (
        slot_table[None, :] == jnp.arange(owners, dtype=jnp.int32)[:, None]
    ).astype(BF16)
    lanes = (((1,), (1,)), ((), ()))
    slot_picks = lax.dot_general(kept, picks, lanes, preferred_element_type=F32)
    slot_gates = lax.dot_general(kept, gates, lanes, preferred_element_type=F32)
    earlier = (jnp.arange(seq_len)[:, None] < jnp.arange(seq_len)[None, :]).astype(BF16)
    before = jnp.dot(slot_picks.astype(BF16), earlier, preferred_element_type=F32)
    lands = (before[:, None, :] == jnp.arange(capacity, dtype=F32)[None, :, None]) & (
        slot_picks[:, None, :] > 0.5
    )
    pick_any = lands.astype(BF16).reshape(owners * capacity, seq_len)
    combine = (
        jnp.where(lands, slot_gates[:, None, :] / 256.0, 0.0)
        .astype(BF16)
        .reshape(owners * capacity, seq_len)
    )
    outgoing = (
        jnp.dot(pick_any, normed, preferred_element_type=jnp.float32)
        .astype(jnp.bfloat16)
        .reshape(owners, capacity, -1)
    )
    incoming = lax.all_to_all(outgoing, "dp", split_axis=0, concat_axis=0, tiled=True)
    routed = incoming.reshape(owners * capacity, -1)
    gate_part = jnp.dot(routed, gate_proj[0], preferred_element_type=jnp.float32)
    up_part = jnp.dot(routed, up_proj[0], preferred_element_type=jnp.float32)
    gate_val, up_val = (
        lax.psum_scatter(
            gate_part.astype(jnp.bfloat16), "tensor", scatter_dimension=1, tiled=True
        ).astype(jnp.float32),
        lax.psum_scatter(
            up_part.astype(jnp.bfloat16), "tensor", scatter_dimension=1, tiled=True
        ).astype(jnp.float32),
    )
    hidden = (jax.nn.silu(gate_val) * up_val).astype(jnp.bfloat16)
    unit_count = hidden.shape[1]
    panel_count = unit_count // PANEL
    split = hidden.reshape(-1, panel_count, PANEL)
    gram = (
        jnp.einsum("rpi,rpj->pij", split, split, preferred_element_type=jnp.float32)
        / routed.shape[0]
    )
    quantized = quantize(down_proj[0], inv_chol[0])
    expert_part = jnp.dot(hidden, quantized, preferred_element_type=jnp.float32)
    expert_rows = lax.psum_scatter(
        expert_part.astype(jnp.bfloat16), "tensor", scatter_dimension=1, tiled=True
    )
    returned = lax.all_to_all(
        expert_rows.reshape(owners, capacity, -1), "dp", split_axis=0, concat_axis=0, tiled=True
    )
    moe = lax.dot_general(
        combine,
        returned.reshape(owners * capacity, -1),
        (((0,), (0,)), ((), ())),
        preferred_element_type=jnp.float32,
    )
    return (
        residual_out,
        moe.astype(jnp.bfloat16),
        quantized[None],
        gram.reshape(unit_count, PANEL)[None],
    )


def solution(mesh):
    placed = (
        P("dp", "tensor"),
        P("dp", "tensor", None),
        P("dp", None),
        P("tensor", None, None),
        P("tensor", "dp"),
        P("tensor"),
        P("dp", None),
        P("dp", None),
        P(),
        P("dp", "tensor", None),
        P("dp", "tensor", None),
        P("dp", "tensor", None),
        P("dp", "tensor", None),
    )
    return jax.shard_map(
        shards,
        mesh=mesh,
        in_specs=placed,
        out_specs=(
            P("dp", "tensor"),
            P("dp", "tensor"),
            P("dp", "tensor", None),
            P("dp", "tensor", None),
        ),
        check_vma=False,
    )
```

```python
import math

import jax
import jax.numpy as jnp
import numpy as np
from jax import lax
from jax.experimental import pallas as pl
from jax.experimental.pallas import tpu as pltpu
from jax.sharding import PartitionSpec as P

D = 7168
NOPE = 128
ROPE = 64
VHEAD = 128
LATENT = 512
PANEL = 128
BLK = 16
CAP = 8
NSUB = 8
LANES = 128
F32 = jnp.float32
BF16 = jnp.bfloat16


def _sin_coeffs():
    n = 400
    u = (0.5 * np.cos(np.pi * (np.arange(n) + 0.5) / (2 * n))) ** 2
    r = np.sqrt(u)
    target = np.sin(2 * np.pi * r) / (2 * np.pi * r)
    vand = np.vander(u, 8, increasing=True)
    return [float(c) for c in np.linalg.lstsq(vand * r[:, None], target * r, rcond=None)[0]]

SINC = _sin_coeffs()

def quantize_panel(us_ref, w_ref, u_ref, sel_ref, q_ref, wnat, cur, err, qi, lo, st, rs, midway):
    tiles = w_ref.shape[1] // (NSUB * LANES)
    width = tiles * LANES
    for c in range(NSUB):
        cols = slice(c * width, (c + 1) * width)
        chunk = w_ref[:, cols].astype(F32)
        wnat[:, cols] = chunk
        low = jnp.min(chunk, axis=0, keepdims=True)
        high = jnp.max(chunk, axis=0, keepdims=True)
        step = (high - low) / 15.0 + 1e-05
        inverse = 1.0 / step
        for j in range(tiles):
            lanes = slice(j * LANES, (j + 1) * LANES)
            lo[j, c:c + 1, :] = low[:, lanes]
            st[j, c:c + 1, :] = step[:, lanes]
            rs[j, c:c + 1, :] = inverse[:, lanes]

    def block(b, first):
        base = pl.multiple_of(b * BLK, BLK)
        for c in range(NSUB):
            for j in range(tiles):
                at = c * width + j * LANES
                cur[j, pl.ds(c, BLK, NSUB), :] = wnat[pl.ds(base, BLK), at:at + LANES]
        low, step, rstep = lo[...], st[...], rs[...]
        for i in range(BLK):
            rows = slice(i * NSUB, (i + 1) * NSUB)
            x = cur[:, rows, :]
            for k in range(i):
                x = x - us_ref[base + k, base + i] * err[:, k * NSUB:(k + 1) * NSUB, :]
            inv = 1.0 / jnp.full((NSUB, LANES), us_ref[base + i, base + i], F32)
            t = jnp.minimum(jnp.maximum((x - low) * rstep, 0.0), 15.0)
            r = t - jnp.floor(t + 0.5)
            v = r * r
            v2 = v * v
            poly = (SINC[0] + SINC[1] * v) + (SINC[2] + SINC[3] * v) * v2
            poly = poly + ((SINC[4] + SINC[5] * v) + (SINC[6] + SINC[7] * v) * v2) * (v2 * v2)
            level = low + step * (t - r * poly)
            err[:, rows, :] = (x - level) * inv[None]
            qi[:, rows, :] = level
        if first is not None:
            parts = jnp.concatenate(split3(u_ref[pl.ds(base, BLK), :]), axis=0)
            coupling = lax.dot_general(
                parts, sel_ref[...], (((0,), (0,)), ((), ())), preferred_element_type=F32
            ).astype(BF16)[first:, :]
        for c in range(NSUB):
            cols = slice(c * width, (c + 1) * width)
            spread = [qi[j, pl.ds(c, BLK, NSUB), :] for j in range(tiles)]
            q_ref[pl.ds(base, BLK), cols] = jnp.concatenate(spread, axis=1).astype(BF16)
            if first is not None:
                spread = [err[j, pl.ds(c, BLK, NSUB), :] for j in range(tiles)]
                e = split3(jnp.concatenate(spread, axis=1))
                stacked = jnp.concatenate([e[p] for p in PART_E], axis=0)
                wnat[first:, cols] = wnat[first:, cols] - jnp.dot(
                    coupling, stacked, preferred_element_type=F32
                )

    def early(b, carry):
        block(b, BLK)
        return carry

    def late(b, carry):
        block(b, 5 * BLK)
        return carry

    lax.fori_loop(0, 4, early, 0)
    midway()
    lax.fori_loop(4, 7, late, 0)
    block(7, None)


PART_U = (0, 0, 0, 1, 1, 2, 1, 2)
PART_E = (0, 1, 2, 0, 1, 0, 2, 1)

def split3(a):
    a1 = a.astype(BF16)
    rest = a - a1.astype(F32)
    a2 = rest.astype(BF16)
    return a1, a2, (rest - a2.astype(F32)).astype(BF16)


def selector():
    sel = np.zeros((3 * BLK, 8 * BLK), np.float32)
    for slot, part in enumerate(PART_U):
        for i in range(BLK):
            sel[part * BLK + i, slot * BLK + i] = 1
    return sel


MESH = pl.DeviceIdType.MESH
SIDE = 4
RING = 8
CHIPS = SIDE * SIDE


def place():
    at = lax.axis_index("dp")
    x = lax.div(at, 2 * SIDE)
    y = lax.rem(lax.div(at, 2), SIDE)
    return x, y, lax.rem(at, 2), lax.axis_index("tensor")


def dp_of(x, y, c):
    return (x * SIDE + y) * 2 + c


def push(src, dst, sems, device):
    return pltpu.make_async_remote_copy(
        src_ref=src, dst_ref=dst, send_sem=sems[0], recv_sem=sems[1], device_id=device,
        device_id_type=MESH,
    )


def greet(device):
    pl.semaphore_signal(
        pltpu.get_barrier_semaphore(), inc=1, device_id=device, device_id_type=MESH
    )


def ring_sum(z, at, ring, send, recv, partial, rows, finish):
    def hop(half, sub, slot):
        to = lax.rem(z + (1 if half == 0 else RING - 1), RING)
        return push(
            ring.at[half, sub, slot],
            ring.at[half, sub, slot + 1],
            (send.at[half, sub, slot], recv.at[half, sub, slot]),
            (at, to),
        )

    def owner(half, step):
        if half == 0:
            return lax.rem(z + 2 * RING - 1 - step, RING)
        return lax.rem(z + 1 + step, RING)

    for half in range(2):
        own = partial(owner(half, 0), half)
        for sub in range(2):
            ring[half, sub, 0] = rows(own, sub).astype(BF16)
            hop(half, sub, 0).start()

    def step(s, carry):
        own = [partial(owner(half, s + 1), half) for half in range(2)]
        for sub in range(2):
            for half in range(2):
                hop(half, sub, s).wait_recv()
                ring[half, sub, s + 1] = (
                    ring[half, sub, s + 1].astype(F32) + rows(own[half], sub)
                ).astype(BF16)
                hop(half, sub, s + 1).start()
        return carry

    lax.fori_loop(0, RING - 2, step, 0)
    own = [partial(z, half) for half in range(2)]
    for sub in range(2):
        for half in range(2):
            hop(half, sub, RING - 2).wait_recv()
            finish(half, sub, ring[half, sub, RING - 1].astype(F32) + rows(own[half], sub))

    def drain(s, carry):
        for sub in range(2):
            for half in range(2):
                hop(half, sub, s).wait_send()
        return carry

    lax.fori_loop(0, RING - 1, drain, 0)


def front_kernel(
    us_ref, w_ref, u_ref, sel_ref, proj_ref, att_ref, res_ref,
    q_ref, out_ref,
    wnat, cur, err, qi, lo, st, rs,
    proj, att, ring, fin, landed,
    proj_send, proj_recv, sib_send, sib_recv, att_send, att_recv,
    ring_send, ring_recv, fin_send, fin_recv,
):
    x, y, c, z = place()
    at = lax.axis_index("dp")
    up_x, down_x = lax.rem(x + 1, SIDE), lax.rem(x + SIDE - 1, SIDE)
    up_y, down_y = lax.rem(y + 1, SIDE), lax.rem(y + SIDE - 1, SIDE)
    far_x, far_y = lax.rem(x + 2, SIDE), lax.rem(y + 2, SIDE)
    x_up, x_down = (dp_of(up_x, y, c), z), (dp_of(down_x, y, c), z)
    y_up, y_down = (dp_of(x, up_y, c), z), (dp_of(x, down_y, c), z)
    sibling = (dp_of(x, y, 1 - c), z)
    z_up, z_down = (at, lax.rem(z + 1, RING)), (at, lax.rem(z + RING - 1, RING))
    pair = lax.div(z, 2) * 2
    bit = lax.rem(z, 2)
    goal_z = pair + lax.div(y, 2)
    goals = [(2 * bit + sub, goal_z) for sub in range(2)]
    sources = [(2 * bit + slot, pair + lax.div(y, 2)) for slot in range(2)]

    def other(who):
        return jnp.logical_not(jnp.logical_and(who[0] == y, who[1] == z))

    for device in (x_up, x_down, y_up, y_down, sibling, z_up, z_down):
        greet(device)
    for who in sources:
        @pl.when(other(who))
        def _():
            greet((dp_of(x, who[0], c), who[1]))
    away = sum(other(who).astype(jnp.int32) for who in goals)
    pl.semaphore_wait(pltpu.get_barrier_semaphore(), 7 + away)

    def sems(send, recv, k):
        return send.at[k], recv.at[k]

    def block(k):
        return proj.at[k * 2 + c]

    half_p, half_a = proj_ref.shape[0] // 2, att_ref.shape[0] // 2
    own_p = [
        push(proj_ref, block(x), sems(proj_send, proj_recv, 0), x_up),
        push(proj_ref, block(x), sems(proj_send, proj_recv, 1), x_down),
        push(proj_ref, block(x), sems(sib_send, sib_recv, 0), sibling),
    ]
    own_a = [
        push(att_ref, att.at[y], sems(att_send, att_recv, 0), y_up),
        push(att_ref, att.at[y], sems(att_send, att_recv, 1), y_down),
    ]
    first = [
        push(proj_ref, block(down_x), sems(proj_send, proj_recv, 0), x_up),
        push(proj_ref, block(up_x), sems(proj_send, proj_recv, 1), x_down),
        push(att_ref, att.at[down_y], sems(att_send, att_recv, 0), y_up),
        push(att_ref, att.at[up_y], sems(att_send, att_recv, 1), y_down),
    ]

    def part(ref, begin, size):
        return ref.at[pl.ds(begin, size)]

    def relay(ref, begin, size, pair_of, device):
        view = part(ref, begin, size)
        return push(view, view, pair_of, device)

    relays = [
        relay(block(down_x), 0, half_p, sems(proj_send, proj_recv, 2), x_up),
        relay(block(up_x), half_p, half_p, sems(proj_send, proj_recv, 3), x_down),
        relay(att.at[down_y], 0, half_a, sems(att_send, att_recv, 2), y_up),
        relay(att.at[up_y], half_a, half_a, sems(att_send, att_recv, 3), y_down),
    ]
    second = [
        relay(block(far_x), 0, half_p, sems(proj_send, proj_recv, 2), x_up),
        relay(block(far_x), half_p, half_p, sems(proj_send, proj_recv, 3), x_down),
        relay(att.at[far_y], 0, half_a, sems(att_send, att_recv, 2), y_up),
        relay(att.at[far_y], half_a, half_a, sems(att_send, att_recv, 3), y_down),
    ]

    def across(k, slot):
        return push(block(k), block(k), sems(sib_send, sib_recv, slot), sibling)

    def from_sibling(k, slot):
        mine = proj.at[k * 2 + 1 - c]
        return push(mine, mine, sems(sib_send, sib_recv, slot), sibling)

    for copy in own_p + own_a:
        copy.start()
    proj[pl.ds(x * 2 + c, 1)] = proj_ref[...][None]
    att[pl.ds(y, 1)] = att_ref[...][None]

    def midway():
        for copy in first:
            copy.wait_recv()
        for copy in relays:
            copy.start()
        across(down_x, 1).start()
        across(up_x, 2).start()

    quantize_panel(
        us_ref, w_ref, u_ref, sel_ref, q_ref, wnat, cur, err, qi, lo, st, rs, midway
    )
    for copy in second:
        copy.wait_recv()
    across(far_x, 3).start()
    for slot, k in enumerate((x, down_x, up_x, far_x)):
        from_sibling(k, slot).wait_recv()

    tokens = att_ref.shape[0]

    def partial(goal, half):
        left = proj[lax.div(goal, 2) * 2 + half]
        right = att[pl.ds(lax.rem(goal, 2) * 2, 2)].reshape(2 * tokens, -1)
        return lax.dot_general(
            left, right, (((1,), (1,)), ((), ())), preferred_element_type=F32
        )

    def rows(value, sub):
        return value[:, sub * tokens:(sub + 1) * tokens]

    def finish(half, sub, value):
        fin[sub, half] = value.astype(BF16)

    ring_sum(z, at, ring, ring_send, ring_recv, partial, rows, finish)

    slot = lax.rem(y, 2)
    for sub, who in enumerate(goals):
        copy = push(
            fin.at[sub], landed.at[slot], (fin_send.at[sub], fin_recv.at[slot]),
            (dp_of(x, who[0], c), who[1]),
        )

        @pl.when(other(who))
        def _():
            copy.start()

        @pl.when(jnp.logical_not(other(who)))
        def _():
            landed[pl.ds(slot, 1)] = fin[sub][None]

    for k, who in enumerate(sources):
        @pl.when(other(who))
        def _():
            push(
                fin.at[0], landed.at[k], (fin_send.at[0], fin_recv.at[k]), sibling
            ).wait_recv()

    total = landed[...].reshape(-1, tokens).astype(F32).T
    out_ref[...] = (res_ref[...].astype(F32) + total).astype(BF16)

    for copy in own_p + own_a + relays:
        copy.wait_send()
    for slot_, k in ((1, down_x), (2, up_x), (3, far_x)):
        across(k, slot_).wait_send()
    for sub, who in enumerate(goals):
        @pl.when(other(who))
        def _():
            push(
                fin.at[sub], landed.at[slot], (fin_send.at[sub], fin_recv.at[slot]), sibling
            ).wait_send()


def front(weight, upper, projection, attended, residual):
    width = weight.shape[1]
    tiles = width // (NSUB * LANES)
    vmem = pl.BlockSpec(memory_space=pltpu.VMEM)
    dma = pltpu.SemaphoreType.DMA
    columns, depth = projection.shape
    tokens = attended.shape[0]
    return pl.pallas_call(
        front_kernel,
        out_shape=(
            jax.ShapeDtypeStruct((PANEL, width), BF16),
            jax.ShapeDtypeStruct(residual.shape, BF16),
        ),
        in_specs=[pl.BlockSpec(memory_space=pltpu.SMEM)] + [vmem] * 6,
        out_specs=(vmem, vmem),
        scratch_shapes=[
            pltpu.VMEM((PANEL, width), F32),
            pltpu.VMEM((tiles, BLK * NSUB, LANES), F32),
            pltpu.VMEM((tiles, BLK * NSUB, LANES), F32),
            pltpu.VMEM((tiles, BLK * NSUB, LANES), F32),
            pltpu.VMEM((tiles, NSUB, LANES), F32),
            pltpu.VMEM((tiles, NSUB, LANES), F32),
            pltpu.VMEM((tiles, NSUB, LANES), F32),
            pltpu.VMEM((2 * SIDE, columns, depth), BF16),
            pltpu.VMEM((SIDE, tokens, depth), BF16),
            pltpu.VMEM((2, 2, RING, columns, tokens), BF16),
            pltpu.VMEM((2, 2, columns, tokens), BF16),
            pltpu.VMEM((2, 2, columns, tokens), BF16),
            dma((4,)), dma((4,)), dma((4,)), dma((4,)), dma((4,)), dma((4,)),
            dma((2, 2, RING)), dma((2, 2, RING)), dma((2,)), dma((2,)),
        ],
        compiler_params=pltpu.CompilerParams(
            vmem_limit_bytes=56 * 2**20, collective_id=0, has_side_effects=True
        ),
        name="front",
    )(
        upper, weight, upper, jnp.asarray(selector(), BF16), projection, attended, residual
    )


def back_kernel(
    res_ref, gain_ref, pick_ref, comb_ref, gate_hbm, up_hbm, q_hbm,
    moe_ref, gram_ref,
    weights, quant, outgoing, incoming, crossing, raw, scaled, square,
    ring_a, hidden, ring_b, rows_out, gathered, returning, returned,
    load_sem, out_send, out_recv, sib_send, sib_recv, sq_send, sq_recv,
    a_send, a_recv, b_send, b_recv, back_send, back_recv,
):
    x, y, c, z = place()
    at = lax.axis_index("dp")
    chip = x * SIDE + y
    sibling = (dp_of(x, y, 1 - c), z)
    loads = [
        pltpu.make_async_copy(gate_hbm, weights.at[0], load_sem.at[0]),
        pltpu.make_async_copy(up_hbm, weights.at[1], load_sem.at[1]),
        pltpu.make_async_copy(q_hbm, quant, load_sem.at[2]),
    ]
    for copy in loads:
        copy.start()

    def chip_at(k):
        return lax.rem(chip + k, CHIPS)

    def greet_chip(k, carry):
        greet((chip_at(k) * 2 + c, z))
        return carry

    def greet_z(k, carry):
        greet((at, lax.rem(z + k, RING)))
        return carry

    lax.fori_loop(1, CHIPS, greet_chip, 0)
    lax.fori_loop(1, RING, greet_z, 0)
    greet(sibling)

    outgoing[...] = jnp.dot(
        pick_ref[...], res_ref[...], preferred_element_type=F32
    ).astype(BF16)
    pl.semaphore_wait(pltpu.get_barrier_semaphore(), CHIPS + RING - 1)

    unit = 2 * CAP

    def exchange(src, dst, send, recv):
        def rows_of(k):
            return pl.ds(pl.multiple_of(k * unit, unit), unit)

        def out(k):
            to = chip_at(k)
            return push(
                src.at[rows_of(to)], dst.at[rows_of(chip)], (send.at[k], recv.at[k]),
                (to * 2 + c, z),
            )

        def come(k):
            here = dst.at[rows_of(chip_at(CHIPS - k))]
            return push(here, here, (send.at[k], recv.at[k]), (chip_at(k) * 2 + c, z))

        def start(k, carry):
            out(k).start()
            return carry

        def arrive(k, carry):
            come(k).wait_recv()
            return carry

        def leave(k, carry):
            out(k).wait_send()
            return carry

        lax.fori_loop(1, CHIPS, start, 0)
        dst[rows_of(chip), :] = src[rows_of(chip), :]
        lax.fori_loop(1, CHIPS, arrive, 0)
        return leave

    leave_out = exchange(outgoing, incoming, out_send, out_recv)

    count = CHIPS * unit
    half = count // 2
    r = lax.broadcasted_iota(jnp.int32, (count, count), 0)
    q = lax.broadcasted_iota(jnp.int32, (count, count), 1)
    spot = ((r >> 3) & 15) * unit + (((r >> 7) ^ c) & 1) * CAP + (r & 7)
    by_core = (q == spot).astype(F32).astype(BF16)
    spot_back = ((q >> 3) & 15) * unit + (((q >> 7) ^ c) & 1) * CAP + (q & 7)
    by_chip = (r == spot_back).astype(F32).astype(BF16)

    both = jnp.dot(by_core, incoming[...], preferred_element_type=F32).astype(BF16)
    raw[0:half, :] = both[:half]
    crossing[...] = both[half:]
    over = push(crossing, raw.at[pl.ds(half, half)], (sib_send.at[0], sib_recv.at[0]), sibling)
    over.start()
    over.wait_recv()

    wide = raw[...].astype(F32)
    square[pl.ds(z, 1)] = lax.dot_general(
        jnp.ones((8, wide.shape[1]), F32), wide * wide, (((1,), (1,)), ((), ())),
        preferred_element_type=F32, precision=lax.Precision.HIGHEST,
    )[None]

    def square_to(k):
        return push(
            square.at[z], square.at[z], (sq_send.at[k], sq_recv.at[k]),
            (at, lax.rem(z + k, RING)),
        )

    def square_from(k):
        here = square.at[lax.rem(z + RING - k, RING)]
        return push(here, here, (sq_send.at[k], sq_recv.at[k]), (at, lax.rem(z + k, RING)))

    def square_start(k, carry):
        square_to(k).start()
        return carry

    def square_arrive(k, carry):
        square_from(k).wait_recv()
        return carry

    def square_leave(k, carry):
        square_to(k).wait_send()
        return carry

    lax.fori_loop(1, RING, square_start, 0)
    scaled[...] = (wide * gain_ref[...].astype(F32)).astype(BF16)
    loads[0].wait()
    loads[1].wait()

    units = hidden.shape[1]
    sums = {}

    def partial_a(goal, side):
        return jnp.dot(
            scaled[...],
            weights[side, :, pl.ds(pl.multiple_of(goal * units, units), units)],
            preferred_element_type=F32,
        )

    def rows_a(value, sub):
        return value[sub * half:(sub + 1) * half]

    def finish_a(side, sub, value):
        sums[side, sub] = value

    ring_sum(z, at, ring_a, a_send, a_recv, partial_a, rows_a, finish_a)

    lax.fori_loop(1, RING, square_arrive, 0)
    mean = jnp.sum(square[...], axis=0) / D
    scale = lax.rsqrt(mean + 1e-06).T[:, 0:1]
    gate = jnp.concatenate([sums[0, 0], sums[0, 1]], axis=0) * scale
    up = jnp.concatenate([sums[1, 0], sums[1, 1]], axis=0) * scale
    hidden[...] = (gate / (1.0 + jnp.exp(-gate)) * up).astype(BF16)
    gram_ref[...] = lax.dot_general(
        hidden[...], hidden[...], (((0,), (0,)), ((), ())), preferred_element_type=F32
    ) / count
    loads[2].wait()

    block = moe_ref.shape[1]

    def partial_b(goal, side):
        return jnp.dot(
            hidden[side * half:(side + 1) * half, :],
            quant[:, pl.ds(pl.multiple_of(goal * block, LANES), block)],
            preferred_element_type=F32,
        )

    part = half // 2

    def rows_b(value, sub):
        return value[sub * part:(sub + 1) * part]

    def finish_b(side, sub, value):
        if side == 0:
            gathered[sub * part:(sub + 1) * part, :] = value.astype(BF16)
        else:
            rows_out[sub * part:(sub + 1) * part, :] = value.astype(BF16)

    ring_sum(z, at, ring_b, b_send, b_recv, partial_b, rows_b, finish_b)

    home = push(
        rows_out, gathered.at[pl.ds(half, half)], (sib_send.at[1], sib_recv.at[1]), sibling
    )
    home.start()
    home.wait_recv()
    returning[...] = jnp.dot(
        by_chip, gathered[...], preferred_element_type=F32
    ).astype(BF16)
    leave_back = exchange(returning, returned, back_send, back_recv)
    moe_ref[...] = lax.dot_general(
        comb_ref[...], returned[...], (((0,), (0,)), ((), ())), preferred_element_type=F32
    ).astype(BF16)

    over.wait_send()
    home.wait_send()
    lax.fori_loop(1, CHIPS, leave_out, 0)
    lax.fori_loop(1, CHIPS, leave_back, 0)
    lax.fori_loop(1, RING, square_leave, 0)


def back(residual, gain, pick_any, combine, gate_w, up_w, quantized):
    vmem = pl.BlockSpec(memory_space=pltpu.VMEM)
    anywhere = pl.BlockSpec(memory_space=pl.ANY)
    dma = pltpu.SemaphoreType.DMA
    tokens, block = residual.shape
    rows = pick_any.shape[0]
    half = rows // 2
    wide = (rows, block)
    return pl.pallas_call(
        back_kernel,
        out_shape=(
            jax.ShapeDtypeStruct((tokens, block), BF16),
            jax.ShapeDtypeStruct((PANEL, PANEL), F32),
        ),
        in_specs=[vmem] * 4 + [anywhere] * 3,
        out_specs=(vmem, vmem),
        scratch_shapes=[
            pltpu.VMEM((2,) + gate_w.shape, BF16),
            pltpu.VMEM(quantized.shape, BF16),
            pltpu.VMEM(wide, BF16),
            pltpu.VMEM(wide, BF16),
            pltpu.VMEM((half, block), BF16),
            pltpu.VMEM(wide, BF16),
            pltpu.VMEM(wide, BF16),
            pltpu.VMEM((RING, 8, rows), F32),
            pltpu.VMEM((2, 2, RING, half, PANEL), BF16),
            pltpu.VMEM((rows, PANEL), BF16),
            pltpu.VMEM((2, 2, RING, half // 2, block), BF16),
            pltpu.VMEM((half, block), BF16),
            pltpu.VMEM(wide, BF16),
            pltpu.VMEM(wide, BF16),
            pltpu.VMEM(wide, BF16),
            dma((3,)), dma((CHIPS,)), dma((CHIPS,)), dma((2,)), dma((2,)), dma((RING,)),
            dma((RING,)), dma((2, 2, RING)), dma((2, 2, RING)), dma((2, 2, RING)),
            dma((2, 2, RING)), dma((CHIPS,)), dma((CHIPS,)),
        ],
        compiler_params=pltpu.CompilerParams(
            vmem_limit_bytes=56 * 2**20, collective_id=1, has_side_effects=True
        ),
        name="back",
    )(residual, gain, pick_any, combine, gate_w, up_w, quantized)


def shards(
    residual_in,
    queries,
    latent,
    latent_up,
    out_proj,
    norm_gain,
    expert_ids,
    gate_num,
    slot_table,
    gate_proj,
    up_proj,
    down_proj,
    inv_chol,
):
    seq_len = queries.shape[0]
    head_count = queries.shape[1]
    scale = 1.0 / math.sqrt(NOPE + ROPE)
    key_value = jnp.einsum(
        "tc,hcd->thd", latent[:, :LATENT], latent_up, preferred_element_type=jnp.float32
    ).astype(jnp.bfloat16)
    rotary = jnp.broadcast_to(latent[:, None, LATENT:], (seq_len, head_count, ROPE))
    keys = jnp.concatenate([key_value[:, :, :NOPE], rotary], axis=2)
    scores = jnp.einsum("thd,shd->hts", queries, keys, preferred_element_type=jnp.float32) * scale
    causal = jnp.arange(seq_len)[None, :] <= jnp.arange(seq_len)[:, None]
    scores = jnp.where(causal[None], scores, -1e30)
    top = jnp.max(scores, axis=2, keepdims=True)
    expo = jnp.exp(scores - top)
    probs = (expo / jnp.sum(expo, axis=2, keepdims=True)).astype(jnp.bfloat16)
    result = jnp.einsum(
        "hts,shd->thd", probs, key_value[:, :, NOPE:], preferred_element_type=jnp.float32
    )
    attended = result.astype(jnp.bfloat16).reshape(seq_len, head_count * VHEAD)
    quantized, residual_out = front(
        down_proj[0], inv_chol[0], out_proj.T, attended, residual_in
    )
    owners = lax.axis_size("dp")
    capacity = CAP
    experts_all = slot_table.shape[0]
    named = expert_ids[:, :, None] == jnp.arange(experts_all, dtype=jnp.int32)[None, None, :]
    picks = jnp.sum(named.astype(F32), axis=1).astype(BF16)
    gates = jnp.sum(jnp.where(named, gate_num[:, :, None], 0), axis=1).astype(BF16)
    kept = (
        slot_table[None, :] == jnp.arange(owners, dtype=jnp.int32)[:, None]
    ).astype(BF16)
    lanes = (((1,), (1,)), ((), ()))
    slot_picks = lax.dot_general(kept, picks, lanes, preferred_element_type=F32)
    slot_gates = lax.dot_general(kept, gates, lanes, preferred_element_type=F32)
    earlier = (jnp.arange(seq_len)[:, None] < jnp.arange(seq_len)[None, :]).astype(BF16)
    before = jnp.dot(slot_picks.astype(BF16), earlier, preferred_element_type=F32)
    lands = (before[:, None, :] == jnp.arange(capacity, dtype=F32)[None, :, None]) & (
        slot_picks[:, None, :] > 0.5
    )
    pick_any = lands.astype(BF16).reshape(owners * capacity, seq_len)
    combine = (
        jnp.where(lands, slot_gates[:, None, :] / 256.0, 0.0)
        .astype(BF16)
        .reshape(owners * capacity, seq_len)
    )
    moe, gram = back(
        residual_out, norm_gain[None], pick_any, combine, gate_proj[0], up_proj[0], quantized
    )
    return residual_out, moe, quantized[None], gram[None]


def solution(mesh):
    placed = (
        P("dp", "tensor"),
        P("dp", "tensor", None),
        P("dp", None),
        P("tensor", None, None),
        P("tensor", "dp"),
        P("tensor"),
        P("dp", None),
        P("dp", None),
        P(),
        P("dp", "tensor", None),
        P("dp", "tensor", None),
        P("dp", "tensor", None),
        P("dp", "tensor", None),
    )
    return jax.shard_map(
        shards,
        mesh=mesh,
        in_specs=placed,
        out_specs=(
            P("dp", "tensor"),
            P("dp", "tensor"),
            P("dp", "tensor", None),
            P("dp", "tensor", None),
        ),
        check_vma=False,
    )
```

```python
import math

import jax
import jax.numpy as jnp
import numpy as np
from jax import lax
from jax.experimental import pallas as pl
from jax.experimental.pallas import tpu as pltpu
from jax.sharding import PartitionSpec as P

D = 7168
NOPE = 128
ROPE = 64
VHEAD = 128
LATENT = 512
PANEL = 128
BLK = 16
CAP = 8
NSUB = 8
LANES = 128
F32 = jnp.float32
BF16 = jnp.bfloat16


def _sin_coeffs():
    n = 400
    u = (0.5 * np.cos(np.pi * (np.arange(n) + 0.5) / (2 * n))) ** 2
    r = np.sqrt(u)
    target = np.sin(2 * np.pi * r) / (2 * np.pi * r)
    vand = np.vander(u, 8, increasing=True)
    return [float(c) for c in np.linalg.lstsq(vand * r[:, None], target * r, rcond=None)[0]]

SINC = _sin_coeffs()

def quantize_panel(us_ref, w_ref, u_ref, sel_ref, q_ref, wnat, cur, err, qi, lo, st, rs):
    tiles = w_ref.shape[1] // (NSUB * LANES)
    width = tiles * LANES

    def ranges():
        for c in range(NSUB):
            cols = slice(c * width, (c + 1) * width)
            chunk = w_ref[:, cols].astype(F32)
            wnat[:, cols] = chunk
            low = jnp.min(chunk, axis=0, keepdims=True)
            high = jnp.max(chunk, axis=0, keepdims=True)
            step = (high - low) / 15.0 + 1e-05
            inverse = 1.0 / step
            for j in range(tiles):
                lanes = slice(j * LANES, (j + 1) * LANES)
                lo[j, c:c + 1, :] = low[:, lanes]
                st[j, c:c + 1, :] = step[:, lanes]
                rs[j, c:c + 1, :] = inverse[:, lanes]

    def block(b, first):
        base = pl.multiple_of(b * BLK, BLK)
        for c in range(NSUB):
            for j in range(tiles):
                at = c * width + j * LANES
                cur[j, pl.ds(c, BLK, NSUB), :] = wnat[pl.ds(base, BLK), at:at + LANES]
        low, step, rstep = lo[...], st[...], rs[...]
        for i in range(BLK):
            rows = slice(i * NSUB, (i + 1) * NSUB)
            x = cur[:, rows, :]
            for k in range(i):
                x = x - us_ref[base + k, base + i] * err[:, k * NSUB:(k + 1) * NSUB, :]
            inv = 1.0 / jnp.full((NSUB, LANES), us_ref[base + i, base + i], F32)
            t = jnp.minimum(jnp.maximum((x - low) * rstep, 0.0), 15.0)
            r = t - jnp.floor(t + 0.5)
            v = r * r
            v2 = v * v
            poly = (SINC[0] + SINC[1] * v) + (SINC[2] + SINC[3] * v) * v2
            poly = poly + ((SINC[4] + SINC[5] * v) + (SINC[6] + SINC[7] * v) * v2) * (v2 * v2)
            level = low + step * (t - r * poly)
            err[:, rows, :] = (x - level) * inv[None]
            qi[:, rows, :] = level
        if first is not None:
            parts = jnp.concatenate(split3(u_ref[pl.ds(base, BLK), :]), axis=0)
            coupling = lax.dot_general(
                parts, sel_ref[...], (((0,), (0,)), ((), ())), preferred_element_type=F32
            ).astype(BF16)[first:, :]
        for c in range(NSUB):
            cols = slice(c * width, (c + 1) * width)
            spread = [qi[j, pl.ds(c, BLK, NSUB), :] for j in range(tiles)]
            q_ref[c, pl.ds(base, BLK), :] = jnp.concatenate(spread, axis=1).astype(BF16)
            if first is not None:
                spread = [err[j, pl.ds(c, BLK, NSUB), :] for j in range(tiles)]
                e = split3(jnp.concatenate(spread, axis=1))
                stacked = jnp.concatenate([e[p] for p in PART_E], axis=0)
                wnat[first:, cols] = wnat[first:, cols] - jnp.dot(
                    coupling, stacked, preferred_element_type=F32
                )

    def early(b, carry):
        block(b, BLK)
        return carry

    def first_half():
        ranges()
        lax.fori_loop(0, 4, early, 0)

    def later(step):
        if isinstance(step, int) and step == 3:
            block(7, None)
        else:
            block(4 + step, 5 * BLK)

    return first_half, later


PART_U = (0, 0, 0, 1, 1, 2, 1, 2)
PART_E = (0, 1, 2, 0, 1, 0, 2, 1)

def split3(a):
    a1 = a.astype(BF16)
    rest = a - a1.astype(F32)
    a2 = rest.astype(BF16)
    return a1, a2, (rest - a2.astype(F32)).astype(BF16)


def selector():
    sel = np.zeros((3 * BLK, 8 * BLK), np.float32)
    for slot, part in enumerate(PART_U):
        for i in range(BLK):
            sel[part * BLK + i, slot * BLK + i] = 1
    return sel


MESH = pl.DeviceIdType.MESH
SIDE = 4
RING = 8
CHIPS = SIDE * SIDE


def place():
    at = lax.axis_index("dp")
    x = lax.div(at, 2 * SIDE)
    y = lax.rem(lax.div(at, 2), SIDE)
    return x, y, lax.rem(at, 2), lax.axis_index("tensor")


def dp_of(x, y, c):
    return (x * SIDE + y) * 2 + c


def push(src, dst, sems, device):
    return pltpu.make_async_remote_copy(
        src_ref=src, dst_ref=dst, send_sem=sems[0], recv_sem=sems[1], device_id=device,
        device_id_type=MESH,
    )


def greet(device):
    pl.semaphore_signal(
        pltpu.get_barrier_semaphore(), inc=1, device_id=device, device_id_type=MESH
    )


def ring_sum(z, at, ring, send, recv, partial, rows, finish, meanwhile=lambda step: None):
    def length(side, half):
        return RING // 2 if side == half else RING // 2 - 1

    def hop(side, half, sub, slot):
        to = lax.rem(z + (1 if side == 0 else RING - 1), RING)
        return push(
            ring.at[side, half, sub, slot],
            ring.at[side, half, sub, slot + 1],
            (send.at[side, half, sub, slot], recv.at[side, half, sub, slot]),
            (at, to),
        )

    def goal(side, half, step):
        away = length(side, half) - step
        return lax.rem(z + (away if side == 0 else RING - away), RING)

    streams = [(0, 0), (1, 1), (0, 1), (1, 0)]
    for side, half in streams:
        own = partial(goal(side, half, 0), half)
        for sub in range(2):
            ring[side, half, sub, 0] = rows(own, sub).astype(BF16)
            hop(side, half, sub, 0).start()
    meanwhile(0)

    def advance(step, members):
        for side, half in members:
            own = partial(goal(side, half, step), half)
            for sub in range(2):
                hop(side, half, sub, step - 1).wait_recv()
                value = rows(own, sub) + ring[side, half, sub, step].astype(F32)
                ring[side, half, sub, step] = value.astype(BF16)
                hop(side, half, sub, step).start()
        meanwhile(step)

    def middle(step, carry):
        advance(step, streams)
        return carry

    lax.fori_loop(1, RING // 2 - 1, middle, 0)
    advance(RING // 2 - 1, streams[:2])
    for half in range(2):
        own = partial(z, half)
        for sub in range(2):
            value = rows(own, sub)
            for side in (1 - half, half):
                last = length(side, half)
                hop(side, half, sub, last - 1).wait_recv()
                value = value + ring[side, half, sub, last].astype(F32)
            finish(half, sub, value)

    def drain():
        def left(step, members):
            for side, half in members:
                for sub in range(2):
                    hop(side, half, sub, step).wait_send()

        def sent(step, carry):
            left(step, streams)
            return carry

        lax.fori_loop(0, RING // 2 - 1, sent, 0)
        left(RING // 2 - 1, streams[:2])

    return drain


def attend(q_ref, latent_ref, up, spread, att_ref):
    tokens, heads = q_ref.shape[0], q_ref.shape[1]
    queries = q_ref[...].astype(F32)
    spread[0] = queries[:, :, :NOPE].reshape(tokens * heads, NOPE)
    blank = jnp.zeros((tokens, heads, NOPE - ROPE), F32)
    spread[1] = jnp.concatenate([queries[:, :, NOPE:], blank], axis=2).reshape(
        tokens * heads, NOPE
    )
    low = latent_ref[:, :LATENT]
    rotary = jnp.concatenate(
        [latent_ref[:, LATENT:].astype(F32), jnp.zeros((tokens, NOPE - ROPE), F32)], axis=1
    ).astype(BF16)
    causal = lax.broadcasted_iota(jnp.int32, (tokens, tokens), 1) <= lax.broadcasted_iota(
        jnp.int32, (tokens, tokens), 0
    )
    for h in range(heads):
        both = jnp.dot(low, up[h], preferred_element_type=F32).astype(BF16)
        query = jnp.concatenate(
            [spread[k, pl.ds(h, tokens, heads), :] for k in range(2)], axis=1
        ).astype(BF16)
        key = jnp.concatenate([both[:, :NOPE], rotary], axis=1)
        scores = lax.dot_general(
            query, key, (((1,), (1,)), ((), ())), preferred_element_type=F32
        ) * (1.0 / math.sqrt(NOPE + ROPE))
        scores = jnp.where(causal, scores, -1e30)
        expo = jnp.exp(scores - jnp.max(scores, axis=1, keepdims=True))
        probs = (expo / jnp.sum(expo, axis=1, keepdims=True)).astype(BF16)
        att_ref[:, h * VHEAD:(h + 1) * VHEAD] = jnp.dot(
            probs, both[:, NOPE:], preferred_element_type=F32
        ).astype(BF16)


def route(ids_ref, num_ref, slot_ref, pick_ref, comb_ref):
    tokens, experts_all = ids_ref.shape[0], slot_ref.shape[1]
    slots = pick_ref.shape[0] // CAP
    names = lax.broadcasted_iota(jnp.int32, (tokens, experts_all), 1)
    picks = jnp.zeros((tokens, experts_all), F32)
    gates = jnp.zeros((tokens, experts_all), F32)
    for k in range(ids_ref.shape[1]):
        hit = ids_ref[:, k:k + 1] == names
        picks = jnp.where(hit, 1.0, picks)
        gates = jnp.where(hit, num_ref[:, k:k + 1].astype(F32), gates)
    kept = jnp.where(
        slot_ref[...] == lax.broadcasted_iota(jnp.int32, (slots, experts_all), 0), 1.0, 0.0
    ).astype(BF16)
    lanes = (((1,), (1,)), ((), ()))
    slot_picks = lax.dot_general(kept, picks.astype(BF16), lanes, preferred_element_type=F32)
    slot_gates = lax.dot_general(kept, gates.astype(BF16), lanes, preferred_element_type=F32)
    earlier = jnp.where(
        lax.broadcasted_iota(jnp.int32, (tokens, tokens), 0)
        < lax.broadcasted_iota(jnp.int32, (tokens, tokens), 1), 1.0, 0.0
    ).astype(BF16)
    before = jnp.dot(slot_picks.astype(BF16), earlier, preferred_element_type=F32)
    before = jnp.where(slot_picks > 0.5, before, -1.0)
    shape = (slots, CAP, tokens)
    spot = lax.broadcasted_iota(jnp.int32, shape, 1).astype(F32)
    lands = jnp.broadcast_to(before[:, None, :], shape) == spot
    weight = jnp.broadcast_to(slot_gates[:, None, :], shape) / 256.0
    pick_ref[...] = jnp.where(lands, 1.0, 0.0).reshape(slots * CAP, tokens).astype(BF16)
    comb_ref[...] = jnp.where(lands, weight, 0.0).reshape(slots * CAP, tokens).astype(BF16)


def front_kernel(
    us_ref, u_ref, sel_ref, proj_ref, res_ref, q_in_ref, latent_ref, ids_ref, num_ref, slot_ref,
    w_hbm, lift_hbm,
    out_ref, pick, comb, q_hbm,
    weight, lift, quant, wnat, cur, err, qi, lo, st, rs,
    spread, att_own, proj, att, ring, fin, landed,
    load_sem, proj_send, proj_recv, cross_send, cross_recv, att_send, att_recv,
    ring_send, ring_recv, fin_send, fin_recv,
):
    x, y, c, z = place()
    at = lax.axis_index("dp")
    up_x, down_x = lax.rem(x + 1, SIDE), lax.rem(x + SIDE - 1, SIDE)
    up_y, down_y = lax.rem(y + 1, SIDE), lax.rem(y + SIDE - 1, SIDE)
    far_x, far_y = lax.rem(x + 2, SIDE), lax.rem(y + 2, SIDE)
    x_up, x_down = (dp_of(up_x, y, c), z), (dp_of(down_x, y, c), z)
    y_up, y_down = (dp_of(x, up_y, c), z), (dp_of(x, down_y, c), z)
    sibling = (dp_of(x, y, 1 - c), z)
    pair = lax.div(z, 2) * 2
    bit = lax.rem(z, 2)
    goal_z = pair + lax.div(y, 2)
    goals = [(2 * bit + sub, goal_z) for sub in range(2)]
    sources = [(2 * bit + slot, goal_z) for slot in range(2)]

    def other(who):
        return jnp.logical_not(jnp.logical_and(who[0] == y, who[1] == z))

    for device in (
        x_up, x_down, y_up, y_down, sibling,
        (at, lax.rem(z + 1, RING)), (at, lax.rem(z + RING - 1, RING)),
    ):
        greet(device)
    for who in sources:
        @pl.when(other(who))
        def _():
            greet((dp_of(x, who[0], c), who[1]))
    loads = [
        pltpu.make_async_copy(lift_hbm, lift, load_sem.at[0]),
        pltpu.make_async_copy(w_hbm, weight, load_sem.at[1]),
    ]
    for copy in loads:
        copy.start()
    away = sum(other(who).astype(jnp.int32) for who in goals)
    pl.semaphore_wait(pltpu.get_barrier_semaphore(), 7 + away)

    def sems(send, recv, k):
        return send.at[k], recv.at[k]

    def block(k):
        return proj.at[k * 2 + c]

    def part(ref, begin, size):
        return ref.at[pl.ds(begin, size)]

    half_p, half_a = proj_ref.shape[0] // 2, att_own.shape[0] // 2
    begins = (0, half_p, half_p, 0)
    own_p = [
        push(
            part(proj_ref, begins[k], half_p), part(block(x), begins[k], half_p),
            sems(proj_send, proj_recv, k), (x_up, x_down)[k % 2],
        )
        for k in range(4)
    ]
    from_p = [
        push(
            part(proj_ref, begins[k], half_p),
            part(block((down_x, up_x)[k % 2]), begins[k], half_p),
            sems(proj_send, proj_recv, k), (x_up, x_down)[k % 2],
        )
        for k in range(4)
    ]

    def relay(ref, begin, size, pair_of, device):
        view = part(ref, begin, size)
        return push(view, view, pair_of, device)

    relay_p = [
        relay(block(down_x), 0, half_p, sems(proj_send, proj_recv, 4), x_up),
        relay(block(up_x), half_p, half_p, sems(proj_send, proj_recv, 5), x_down),
    ]
    far_p = [
        relay(block(far_x), 0, half_p, sems(proj_send, proj_recv, 4), x_up),
        relay(block(far_x), half_p, half_p, sems(proj_send, proj_recv, 5), x_down),
    ]
    own_across = push(proj_ref, block(x), sems(cross_send, cross_recv, 0), sibling)

    def across(k, slot):
        return push(block(k), block(k), sems(cross_send, cross_recv, slot), sibling)

    def from_sibling(k, slot):
        mine = proj.at[k * 2 + 1 - c]
        return push(mine, mine, sems(cross_send, cross_recv, slot), sibling)

    for copy in own_p:
        copy.start()
    own_across.start()

    loads[0].wait()
    attend(q_in_ref, latent_ref, lift, spread, att_own)

    own_a = [
        push(att_own, att.at[y], sems(att_send, att_recv, 0), y_up),
        push(att_own, att.at[y], sems(att_send, att_recv, 1), y_down),
    ]
    from_a = [
        push(att_own, att.at[down_y], sems(att_send, att_recv, 0), y_up),
        push(att_own, att.at[up_y], sems(att_send, att_recv, 1), y_down),
    ]
    relay_a = [
        relay(att.at[down_y], 0, half_a, sems(att_send, att_recv, 2), y_up),
        relay(att.at[up_y], half_a, half_a, sems(att_send, att_recv, 3), y_down),
    ]
    far_a = [
        relay(att.at[far_y], 0, half_a, sems(att_send, att_recv, 2), y_up),
        relay(att.at[far_y], half_a, half_a, sems(att_send, att_recv, 3), y_down),
    ]
    for copy in own_a:
        copy.start()
    for k in range(2):
        from_p[k].wait_recv()
        relay_p[k].start()
    proj[pl.ds(x * 2 + c, 1)] = proj_ref[...][None]
    att[pl.ds(y, 1)] = att_own[...][None]
    route(ids_ref, num_ref, slot_ref, pick, comb)
    for k in range(2, 4):
        from_p[k].wait_recv()
    across(down_x, 1).start()
    across(up_x, 2).start()
    for copy in from_a:
        copy.wait_recv()
    for copy in relay_a:
        copy.start()
    loads[1].wait()
    quantize_first, quantize_later = quantize_panel(
        us_ref, weight, u_ref, sel_ref, quant, wnat, cur, err, qi, lo, st, rs
    )
    quantize_first()
    for copy in far_p:
        copy.wait_recv()
    across(far_x, 3).start()
    for copy in far_a:
        copy.wait_recv()
    for slot, k in enumerate((x, down_x, up_x, far_x)):
        from_sibling(k, slot).wait_recv()

    tokens = att_own.shape[0]

    def partial(goal, half):
        left = proj[lax.div(goal, 2) * 2 + half]
        right = att[pl.ds(lax.rem(goal, 2) * 2, 2)].reshape(2 * tokens, -1)
        return lax.dot_general(
            left, right, (((1,), (1,)), ((), ())), preferred_element_type=F32
        )

    def rows(value, sub):
        return value[:, sub * tokens:(sub + 1) * tokens]

    my_slot = lax.rem(y, 2)

    def deliver(half, sub):
        who = goals[sub]
        return push(
            fin.at[sub, half], landed.at[my_slot, half],
            (fin_send.at[sub, half], fin_recv.at[my_slot, half]),
            (dp_of(x, who[0], c), who[1]),
        )

    def finish(half, sub, value):
        fin[sub, half] = value.astype(BF16)

        @pl.when(other(goals[sub]))
        def _():
            deliver(half, sub).start()

        @pl.when(jnp.logical_not(other(goals[sub])))
        def _():
            landed[pl.ds(my_slot, 1), half] = value.astype(BF16)[None]

    drain = ring_sum(
        z, at, ring, ring_send, ring_recv, partial, rows, finish, quantize_later
    )
    width = res_ref.shape[1]
    q_out = [
        pltpu.make_async_copy(
            quant.at[k], q_hbm.at[:, pl.ds(k * width, width)], load_sem.at[2 + k]
        )
        for k in range(NSUB)
    ]
    for copy in q_out:
        copy.start()
    drain()
    for slot, who in enumerate(sources):
        @pl.when(other(who))
        def _():
            for half in range(2):
                push(
                    fin.at[0, half], landed.at[slot, half],
                    (fin_send.at[0, half], fin_recv.at[slot, half]), sibling,
                ).wait_recv()

    total = landed[...].reshape(-1, tokens).astype(F32).T
    out_ref[...] = (res_ref[...].astype(F32) + total).astype(BF16)
    for copy in own_p + relay_p + own_a + relay_a + [own_across]:
        copy.wait_send()
    for slot, k in ((1, down_x), (2, up_x), (3, far_x)):
        across(k, slot).wait_send()
    for sub, who in enumerate(goals):
        @pl.when(other(who))
        def _():
            for side in range(2):
                deliver(side, sub).wait_send()
    for copy in q_out:
        copy.wait()


def back_kernel(
    res_ref, gain_ref, pick, comb, gate_hbm, up_hbm, q_hbm,
    moe_ref, gram_ref,
    weights, quant, outgoing, incoming, crossing, raw, scaled, square,
    ring_a, hidden, ring_b, rows_out, gathered, returning, returned,
    load_sem, out_send, out_recv, sib_send, sib_recv, sq_send, sq_recv,
    a_send, a_recv, b_send, b_recv, back_send, back_recv,
):
    x, y, c, z = place()
    at = lax.axis_index("dp")
    chip = x * SIDE + y
    sibling = (dp_of(x, y, 1 - c), z)

    def chip_at(k):
        return lax.rem(chip + k, CHIPS)

    def greet_chip(k, carry):
        greet((chip_at(k) * 2 + c, z))
        return carry

    def greet_z(k, carry):
        greet((at, lax.rem(z + k, RING)))
        return carry

    lax.fori_loop(1, CHIPS, greet_chip, 0)
    lax.fori_loop(1, RING, greet_z, 0)
    greet(sibling)
    width = res_ref.shape[1]
    loads = [
        pltpu.make_async_copy(gate_hbm, weights.at[0], load_sem.at[0]),
        pltpu.make_async_copy(up_hbm, weights.at[1], load_sem.at[1]),
    ] + [
        pltpu.make_async_copy(
            q_hbm.at[:, pl.ds(k * width, width)], quant.at[k], load_sem.at[2 + k]
        )
        for k in range(NSUB)
    ]
    for copy in loads:
        copy.start()
    outgoing[...] = jnp.dot(pick[...], res_ref[...], preferred_element_type=F32).astype(BF16)
    pl.semaphore_wait(pltpu.get_barrier_semaphore(), CHIPS + RING - 1)

    unit = 2 * CAP

    def exchange(src, dst, send, recv, meanwhile):
        def rows_of(k):
            return pl.ds(pl.multiple_of(k * unit, unit), unit)

        def out(k):
            to = chip_at(k)
            return push(
                src.at[rows_of(to)], dst.at[rows_of(chip)], (send.at[k], recv.at[k]),
                (to * 2 + c, z),
            )

        def come(k):
            here = dst.at[rows_of(chip_at(CHIPS - k))]
            return push(here, here, (send.at[k], recv.at[k]), (chip_at(k) * 2 + c, z))

        def start(k, carry):
            out(k).start()
            return carry

        def arrive(k, carry):
            come(k).wait_recv()
            return carry

        def leave(k, carry):
            out(k).wait_send()
            return carry

        lax.fori_loop(1, CHIPS, start, 0)
        dst[rows_of(chip), :] = src[rows_of(chip), :]
        meanwhile()
        lax.fori_loop(1, CHIPS, arrive, 0)
        return leave

    leave_out = exchange(outgoing, incoming, out_send, out_recv, lambda: None)

    count = CHIPS * unit
    half = count // 2
    r = lax.broadcasted_iota(jnp.int32, (count, count), 0)
    q = lax.broadcasted_iota(jnp.int32, (count, count), 1)
    spot = ((r >> 3) & 15) * unit + (((r >> 7) ^ c) & 1) * CAP + (r & 7)
    by_core = (q == spot).astype(F32).astype(BF16)
    spot_back = ((q >> 3) & 15) * unit + (((q >> 7) ^ c) & 1) * CAP + (q & 7)
    by_chip = (r == spot_back).astype(F32).astype(BF16)

    both = jnp.dot(by_core, incoming[...], preferred_element_type=F32).astype(BF16)
    raw[0:half, :] = both[:half]
    crossing[...] = both[half:]
    over = push(crossing, raw.at[pl.ds(half, half)], (sib_send.at[0], sib_recv.at[0]), sibling)
    over.start()
    over.wait_recv()

    wide = raw[...].astype(F32)
    square[pl.ds(z, 1)] = lax.dot_general(
        jnp.ones((8, wide.shape[1]), F32), wide * wide, (((1,), (1,)), ((), ())),
        preferred_element_type=F32, precision=lax.Precision.HIGHEST,
    )[None]

    def square_to(k):
        return push(
            square.at[z], square.at[z], (sq_send.at[k], sq_recv.at[k]),
            (at, lax.rem(z + k, RING)),
        )

    def square_from(k):
        here = square.at[lax.rem(z + RING - k, RING)]
        return push(here, here, (sq_send.at[k], sq_recv.at[k]), (at, lax.rem(z + k, RING)))

    def square_start(k, carry):
        square_to(k).start()
        return carry

    def square_arrive(k, carry):
        square_from(k).wait_recv()
        return carry

    def square_leave(k, carry):
        square_to(k).wait_send()
        return carry

    lax.fori_loop(1, RING, square_start, 0)
    scaled[...] = (wide * gain_ref[...].astype(F32)).astype(BF16)
    loads[0].wait()
    loads[1].wait()

    units = hidden.shape[1]
    sums = {}

    def partial_a(goal, side):
        return jnp.dot(
            scaled[...],
            weights[side, :, pl.ds(pl.multiple_of(goal * units, units), units)],
            preferred_element_type=F32,
        )

    def rows_a(value, sub):
        return value[sub * half:(sub + 1) * half]

    def finish_a(side, sub, value):
        sums[side, sub] = value

    drain_a = ring_sum(z, at, ring_a, a_send, a_recv, partial_a, rows_a, finish_a)

    lax.fori_loop(1, RING, square_arrive, 0)
    mean = jnp.sum(square[...], axis=0) / D
    scale = lax.rsqrt(mean + 1e-06).T[:, 0:1]
    gate = jnp.concatenate([sums[0, 0], sums[0, 1]], axis=0) * scale
    up = jnp.concatenate([sums[1, 0], sums[1, 1]], axis=0) * scale
    hidden[...] = (gate / (1.0 + jnp.exp(-gate)) * up).astype(BF16)
    gram_ref[...] = lax.dot_general(
        hidden[...], hidden[...], (((0,), (0,)), ((), ())), preferred_element_type=F32
    ) / count


    def partial_b(goal, side):
        return goal, side

    quarter = half // 2

    def rows_b(value, sub):
        goal, side = value
        begin = side * half + sub * quarter
        return jnp.dot(
            hidden[begin:begin + quarter, :], quant[goal], preferred_element_type=F32
        )

    def finish_b(side, sub, value):
        if side == 0:
            gathered[sub * quarter:(sub + 1) * quarter, :] = value.astype(BF16)
        else:
            rows_out[sub * quarter:(sub + 1) * quarter, :] = value.astype(BF16)

    for copy in loads[2:]:
        copy.wait()
    drain_b = ring_sum(z, at, ring_b, b_send, b_recv, partial_b, rows_b, finish_b)


    home = push(
        rows_out, gathered.at[pl.ds(half, half)], (sib_send.at[1], sib_recv.at[1]), sibling
    )
    home.start()
    home.wait_recv()
    returning[...] = jnp.dot(
        by_chip, gathered[...], preferred_element_type=F32
    ).astype(BF16)
    def settle():
        drain_a()
        drain_b()
        lax.fori_loop(1, CHIPS, leave_out, 0)
        lax.fori_loop(1, RING, square_leave, 0)

    leave_back = exchange(returning, returned, back_send, back_recv, settle)
    moe_ref[...] = lax.dot_general(
        comb[...], returned[...], (((0,), (0,)), ((), ())), preferred_element_type=F32
    ).astype(BF16)

    over.wait_send()
    home.wait_send()
    lax.fori_loop(1, CHIPS, leave_back, 0)
def front(us, projection, residual, queries, latent, ids, num, slots, weight, lift):
    width = weight.shape[1]
    tiles = width // (NSUB * LANES)
    vmem = pl.BlockSpec(memory_space=pltpu.VMEM)
    anywhere = pl.BlockSpec(memory_space=pl.ANY)
    dma = pltpu.SemaphoreType.DMA
    columns, depth = projection.shape
    tokens, block = residual.shape
    heads = queries.shape[1]
    rows = 2 * CAP * CHIPS
    meet = (2, 2, 2, RING // 2)
    return pl.pallas_call(
        front_kernel,
        out_shape=(
            jax.ShapeDtypeStruct((tokens, block), BF16),
            jax.ShapeDtypeStruct((rows, tokens), BF16),
            jax.ShapeDtypeStruct((rows, tokens), BF16),
            jax.ShapeDtypeStruct((PANEL, width), BF16),
        ),
        in_specs=[pl.BlockSpec(memory_space=pltpu.SMEM)] + [vmem] * 9 + [anywhere] * 2,
        out_specs=(vmem, vmem, vmem, anywhere),
        scratch_shapes=[
            pltpu.VMEM((PANEL, width), BF16),
            pltpu.VMEM(lift.shape, BF16),
            pltpu.VMEM((NSUB, PANEL, width // NSUB), BF16),
            pltpu.VMEM((PANEL, width), F32),
            pltpu.VMEM((tiles, BLK * NSUB, LANES), F32),
            pltpu.VMEM((tiles, BLK * NSUB, LANES), F32),
            pltpu.VMEM((tiles, BLK * NSUB, LANES), F32),
            pltpu.VMEM((tiles, NSUB, LANES), F32),
            pltpu.VMEM((tiles, NSUB, LANES), F32),
            pltpu.VMEM((tiles, NSUB, LANES), F32),
            pltpu.VMEM((2, tokens * heads, NOPE), F32),
            pltpu.VMEM((tokens, depth), BF16),
            pltpu.VMEM((2 * SIDE, columns, depth), BF16),
            pltpu.VMEM((SIDE, tokens, depth), BF16),
            pltpu.VMEM((2, 2, 2, RING // 2 + 1, columns, tokens), BF16),
            pltpu.VMEM((2, 2, columns, tokens), BF16),
            pltpu.VMEM((2, 2, columns, tokens), BF16),
            dma((2 + NSUB,)), dma((6,)), dma((6,)), dma((4,)), dma((4,)), dma((4,)), dma((4,)),
            dma(meet), dma(meet), dma((2, 2)), dma((2, 2)),
        ],
        compiler_params=pltpu.CompilerParams(
            vmem_limit_bytes=56 * 2**20, collective_id=0, has_side_effects=True
        ),
        name="front",
    )(
        us, us, jnp.asarray(selector(), BF16), projection, residual, queries, latent, ids, num,
        slots, weight, lift,
    )


def back(residual, gain, pick_any, combine, gate_w, up_w, quantized):
    vmem = pl.BlockSpec(memory_space=pltpu.VMEM)
    anywhere = pl.BlockSpec(memory_space=pl.ANY)
    dma = pltpu.SemaphoreType.DMA
    tokens, block = residual.shape
    rows = pick_any.shape[0]
    half = rows // 2
    wide = (rows, block)
    meet = (2, 2, 2, RING // 2)
    slots_of = (2, 2, 2, RING // 2 + 1)
    return pl.pallas_call(
        back_kernel,
        out_shape=(
            jax.ShapeDtypeStruct((tokens, block), BF16),
            jax.ShapeDtypeStruct((PANEL, PANEL), F32),
        ),
        in_specs=[vmem] * 4 + [anywhere] * 3,
        out_specs=(vmem, vmem),
        scratch_shapes=[
            pltpu.VMEM((2,) + gate_w.shape, BF16),
            pltpu.VMEM((NSUB, PANEL, block), BF16),
            pltpu.VMEM(wide, BF16),
            pltpu.VMEM(wide, BF16),
            pltpu.VMEM((half, block), BF16),
            pltpu.VMEM(wide, BF16),
            pltpu.VMEM(wide, BF16),
            pltpu.VMEM((RING, 8, rows), F32),
            pltpu.VMEM(slots_of + (half, PANEL), BF16),
            pltpu.VMEM((rows, PANEL), BF16),
            pltpu.VMEM(slots_of + (half // 2, block), BF16),
            pltpu.VMEM((half, block), BF16),
            pltpu.VMEM(wide, BF16),
            pltpu.VMEM(wide, BF16),
            pltpu.VMEM(wide, BF16),
            dma((2 + NSUB,)), dma((CHIPS,)), dma((CHIPS,)), dma((2,)), dma((2,)), dma((RING,)),
            dma((RING,)), dma(meet), dma(meet), dma(meet), dma(meet), dma((CHIPS,)),
            dma((CHIPS,)),
        ],
        compiler_params=pltpu.CompilerParams(
            vmem_limit_bytes=56 * 2**20, collective_id=1, has_side_effects=True
        ),
        name="back",
    )(residual, gain, pick_any, combine, gate_w, up_w, quantized)


def shards(
    residual_in,
    queries,
    latent,
    latent_up,
    out_proj,
    norm_gain,
    expert_ids,
    gate_num,
    slot_table,
    gate_proj,
    up_proj,
    down_proj,
    inv_chol,
):
    residual_out, pick_any, combine, quantized = front(
        inv_chol[0], out_proj.T, residual_in, queries, latent, expert_ids, gate_num,
        slot_table[None], down_proj[0], latent_up,
    )
    moe, gram = back(
        residual_out, norm_gain[None], pick_any, combine, gate_proj[0], up_proj[0], quantized
    )
    return residual_out, moe, quantized[None], gram[None]


def solution(mesh):
    placed = (
        P("dp", "tensor"),
        P("dp", "tensor", None),
        P("dp", None),
        P("tensor", None, None),
        P("tensor", "dp"),
        P("tensor"),
        P("dp", None),
        P("dp", None),
        P(),
        P("dp", "tensor", None),
        P("dp", "tensor", None),
        P("dp", "tensor", None),
        P("dp", "tensor", None),
    )
    return jax.shard_map(
        shards,
        mesh=mesh,
        in_specs=placed,
        out_specs=(
            P("dp", "tensor"),
            P("dp", "tensor"),
            P("dp", "tensor", None),
            P("dp", "tensor", None),
        ),
        check_vma=False,
    )
```

```python
import math

import jax
import jax.numpy as jnp
import numpy as np
from jax import lax
from jax.experimental import pallas as pl
from jax.experimental.pallas import tpu as pltpu
from jax.sharding import PartitionSpec as P

D = 7168
NOPE = 128
ROPE = 64
VHEAD = 128
LATENT = 512
PANEL = 128
BLK = 16
CAP = 8
NSUB = 8
LANES = 128
F32 = jnp.float32
BF16 = jnp.bfloat16


def _sin_coeffs():
    n = 400
    u = (0.5 * np.cos(np.pi * (np.arange(n) + 0.5) / (2 * n))) ** 2
    r = np.sqrt(u)
    target = np.sin(2 * np.pi * r) / (2 * np.pi * r)
    vand = np.vander(u, 8, increasing=True)
    return [float(c) for c in np.linalg.lstsq(vand * r[:, None], target * r, rcond=None)[0]]

SINC = _sin_coeffs()

def quantize_panel(us_ref, w_ref, u_ref, sel_ref, q_ref, wnat, cur, err, qi, lo, st, rs):
    tiles = w_ref.shape[1] // (NSUB * LANES)
    width = tiles * LANES

    def ranges():
        for c in range(NSUB):
            cols = slice(c * width, (c + 1) * width)
            chunk = w_ref[:, cols].astype(F32)
            wnat[:, cols] = chunk
            low = jnp.min(chunk, axis=0, keepdims=True)
            high = jnp.max(chunk, axis=0, keepdims=True)
            step = (high - low) / 15.0 + 1e-05
            inverse = 1.0 / step
            for j in range(tiles):
                lanes = slice(j * LANES, (j + 1) * LANES)
                lo[j, c:c + 1, :] = low[:, lanes]
                st[j, c:c + 1, :] = step[:, lanes]
                rs[j, c:c + 1, :] = inverse[:, lanes]

    def block(b, first):
        base = pl.multiple_of(b * BLK, BLK)
        for c in range(NSUB):
            for j in range(tiles):
                at = c * width + j * LANES
                cur[j, pl.ds(c, BLK, NSUB), :] = wnat[pl.ds(base, BLK), at:at + LANES]
        low, step, rstep = lo[...], st[...], rs[...]
        for i in range(BLK):
            rows = slice(i * NSUB, (i + 1) * NSUB)
            x = cur[:, rows, :]
            for k in range(i):
                x = x - us_ref[base + k, base + i] * err[:, k * NSUB:(k + 1) * NSUB, :]
            inv = 1.0 / jnp.full((NSUB, LANES), us_ref[base + i, base + i], F32)
            t = jnp.minimum(jnp.maximum((x - low) * rstep, 0.0), 15.0)
            r = t - jnp.floor(t + 0.5)
            v = r * r
            v2 = v * v
            poly = (SINC[0] + SINC[1] * v) + (SINC[2] + SINC[3] * v) * v2
            poly = poly + ((SINC[4] + SINC[5] * v) + (SINC[6] + SINC[7] * v) * v2) * (v2 * v2)
            level = low + step * (t - r * poly)
            err[:, rows, :] = (x - level) * inv[None]
            qi[:, rows, :] = level
        if first is not None:
            parts = jnp.concatenate(split3(u_ref[pl.ds(base, BLK), :]), axis=0)
            coupling = lax.dot_general(
                parts, sel_ref[...], (((0,), (0,)), ((), ())), preferred_element_type=F32
            ).astype(BF16)[first:, :]
        for c in range(NSUB):
            cols = slice(c * width, (c + 1) * width)
            spread = [qi[j, pl.ds(c, BLK, NSUB), :] for j in range(tiles)]
            q_ref[c, pl.ds(base, BLK), :] = jnp.concatenate(spread, axis=1).astype(BF16)
            if first is not None:
                spread = [err[j, pl.ds(c, BLK, NSUB), :] for j in range(tiles)]
                e = split3(jnp.concatenate(spread, axis=1))
                stacked = jnp.concatenate([e[p] for p in PART_E], axis=0)
                wnat[first:, cols] = wnat[first:, cols] - jnp.dot(
                    coupling, stacked, preferred_element_type=F32
                )

    def early(b, carry):
        block(b, BLK)
        return carry

    def first_half(begin, end):
        if begin == 0:
            ranges()
        lax.fori_loop(begin, end, early, 0)

    def later(step):
        if isinstance(step, int) and step == 3:
            block(7, None)
        else:
            block(4 + step, 5 * BLK)

    return first_half, later


PART_U = (0, 0, 0, 1, 1, 2, 1, 2)
PART_E = (0, 1, 2, 0, 1, 0, 2, 1)

def split3(a):
    a1 = a.astype(BF16)
    rest = a - a1.astype(F32)
    a2 = rest.astype(BF16)
    return a1, a2, (rest - a2.astype(F32)).astype(BF16)


def selector():
    sel = np.zeros((3 * BLK, 8 * BLK), np.float32)
    for slot, part in enumerate(PART_U):
        for i in range(BLK):
            sel[part * BLK + i, slot * BLK + i] = 1
    return sel


MESH = pl.DeviceIdType.MESH
SIDE = 4
RING = 8
CHIPS = SIDE * SIDE


def place():
    at = lax.axis_index("dp")
    x = lax.div(at, 2 * SIDE)
    y = lax.rem(lax.div(at, 2), SIDE)
    return x, y, lax.rem(at, 2), lax.axis_index("tensor")


def dp_of(x, y, c):
    return (x * SIDE + y) * 2 + c


def push(src, dst, sems, device):
    return pltpu.make_async_remote_copy(
        src_ref=src, dst_ref=dst, send_sem=sems[0], recv_sem=sems[1], device_id=device,
        device_id_type=MESH,
    )


def greet(device):
    pl.semaphore_signal(
        pltpu.get_barrier_semaphore(), inc=1, device_id=device, device_id_type=MESH
    )


def ring_sum(z, at, ring, send, recv, partial, rows, finish, meanwhile=lambda step: None):
    def length(side, half):
        return RING // 2 if side == half else RING // 2 - 1

    def hop(side, half, sub, slot):
        to = lax.rem(z + (1 if side == 0 else RING - 1), RING)
        return push(
            ring.at[side, half, sub, slot],
            ring.at[side, half, sub, slot + 1],
            (send.at[side, half, sub, slot], recv.at[side, half, sub, slot]),
            (at, to),
        )

    def goal(side, half, step):
        away = length(side, half) - step
        return lax.rem(z + (away if side == 0 else RING - away), RING)

    streams = [(0, 0), (1, 1), (0, 1), (1, 0)]
    for side, half in streams:
        own = partial(goal(side, half, 0), half)
        for sub in range(2):
            ring[side, half, sub, 0] = rows(own, sub).astype(BF16)
            hop(side, half, sub, 0).start()
    meanwhile(0)

    def advance(step, members):
        for side, half in members:
            own = partial(goal(side, half, step), half)
            for sub in range(2):
                hop(side, half, sub, step - 1).wait_recv()
                value = rows(own, sub) + ring[side, half, sub, step].astype(F32)
                ring[side, half, sub, step] = value.astype(BF16)
                hop(side, half, sub, step).start()
        meanwhile(step)

    def middle(step, carry):
        advance(step, streams)
        return carry

    lax.fori_loop(1, RING // 2 - 1, middle, 0)
    advance(RING // 2 - 1, streams[:2])
    for half in range(2):
        own = partial(z, half)
        for sub in range(2):
            value = rows(own, sub)
            for side in (1 - half, half):
                last = length(side, half)
                hop(side, half, sub, last - 1).wait_recv()
                value = value + ring[side, half, sub, last].astype(F32)
            finish(half, sub, value)

    def drain():
        def left(step, members):
            for side, half in members:
                for sub in range(2):
                    hop(side, half, sub, step).wait_send()

        def sent(step, carry):
            left(step, streams)
            return carry

        lax.fori_loop(0, RING // 2 - 1, sent, 0)
        left(RING // 2 - 1, streams[:2])

    return drain


def attend(q_ref, latent_ref, up, att_ref):
    heads, tokens = q_ref.shape[0], q_ref.shape[2]
    rows = (((0,), (0,)), ((), ()))
    low = latent_ref[:LATENT, :]
    rotary = latent_ref[LATENT:, :]
    causal = lax.broadcasted_iota(jnp.int32, (tokens, tokens), 1) <= lax.broadcasted_iota(
        jnp.int32, (tokens, tokens), 0
    )
    for h in range(heads):
        both = lax.dot_general(up[h], low, rows, preferred_element_type=F32).astype(BF16)
        key = jnp.concatenate([both[:NOPE], rotary], axis=0)
        scores = lax.dot_general(q_ref[h], key, rows, preferred_element_type=F32) * (
            1.0 / math.sqrt(NOPE + ROPE)
        )
        scores = jnp.where(causal, scores, -1e30)
        expo = jnp.exp(scores - jnp.max(scores, axis=1, keepdims=True))
        probs = (expo / jnp.sum(expo, axis=1, keepdims=True)).astype(BF16)
        att_ref[:, h * VHEAD:(h + 1) * VHEAD] = lax.dot_general(
            probs, both[NOPE:], (((1,), (1,)), ((), ())), preferred_element_type=F32
        ).astype(BF16)


def route(ids_ref, num_ref, slot_ref, pick_ref, comb_ref):
    tokens, experts_all = ids_ref.shape[1], slot_ref.shape[1]
    slots = pick_ref.shape[0] // CAP
    names = lax.broadcasted_iota(jnp.int32, (experts_all, tokens), 0)
    picks = jnp.zeros((experts_all, tokens), F32)
    gates = jnp.zeros((experts_all, tokens), F32)
    for k in range(ids_ref.shape[0]):
        hit = ids_ref[k:k + 1, :] == names
        picks = jnp.where(hit, 1.0, picks)
        gates = jnp.where(hit, num_ref[k:k + 1, :].astype(F32), gates)
    kept = jnp.where(
        slot_ref[...] == lax.broadcasted_iota(jnp.int32, (slots, experts_all), 0), 1.0, 0.0
    ).astype(BF16)
    slot_picks = jnp.dot(kept, picks.astype(BF16), preferred_element_type=F32)
    slot_gates = jnp.dot(kept, gates.astype(BF16), preferred_element_type=F32)
    earlier = jnp.where(
        lax.broadcasted_iota(jnp.int32, (tokens, tokens), 0)
        < lax.broadcasted_iota(jnp.int32, (tokens, tokens), 1), 1.0, 0.0
    ).astype(BF16)
    before = jnp.dot(slot_picks.astype(BF16), earlier, preferred_element_type=F32)
    before = jnp.where(slot_picks > 0.5, before, -1.0)
    shape = (slots, CAP, tokens)
    spot = lax.broadcasted_iota(jnp.int32, shape, 1).astype(F32)
    lands = jnp.broadcast_to(before[:, None, :], shape) == spot
    weight = jnp.broadcast_to(slot_gates[:, None, :], shape) / 256.0
    pick_ref[...] = jnp.where(lands, 1.0, 0.0).reshape(slots * CAP, tokens).astype(BF16)
    comb_ref[...] = jnp.where(lands, weight, 0.0).reshape(slots * CAP, tokens).astype(BF16)


def front_kernel(
    us_ref, u_ref, sel_ref, proj_ref, res_ref, q_in_ref, latent_ref, ids_ref, num_ref, slot_ref,
    w_hbm, lift_hbm,
    out_ref, pick, comb, q_hbm,
    weight, lift, quant, wnat, cur, err, qi, lo, st, rs,
    att_own, proj, att, ring, fin, landed,
    load_sem, proj_send, proj_recv, cross_send, cross_recv, att_send, att_recv,
    ring_send, ring_recv, fin_send, fin_recv,
):
    x, y, c, z = place()
    at = lax.axis_index("dp")
    up_x, down_x = lax.rem(x + 1, SIDE), lax.rem(x + SIDE - 1, SIDE)
    up_y, down_y = lax.rem(y + 1, SIDE), lax.rem(y + SIDE - 1, SIDE)
    far_x, far_y = lax.rem(x + 2, SIDE), lax.rem(y + 2, SIDE)
    x_up, x_down = (dp_of(up_x, y, c), z), (dp_of(down_x, y, c), z)
    y_up, y_down = (dp_of(x, up_y, c), z), (dp_of(x, down_y, c), z)
    sibling = (dp_of(x, y, 1 - c), z)
    pair = lax.div(z, 2) * 2
    bit = lax.rem(z, 2)
    goal_z = pair + lax.div(y, 2)
    goals = [(2 * bit + sub, goal_z) for sub in range(2)]
    sources = [(2 * bit + slot, goal_z) for slot in range(2)]

    def other(who):
        return jnp.logical_not(jnp.logical_and(who[0] == y, who[1] == z))

    for device in (
        x_up, x_down, y_up, y_down, sibling,
        (at, lax.rem(z + 1, RING)), (at, lax.rem(z + RING - 1, RING)),
    ):
        greet(device)
    for who in sources:
        @pl.when(other(who))
        def _():
            greet((dp_of(x, who[0], c), who[1]))
    loads = [
        pltpu.make_async_copy(lift_hbm, lift, load_sem.at[0]),
        pltpu.make_async_copy(w_hbm, weight, load_sem.at[1]),
    ]
    for copy in loads:
        copy.start()
    away = sum(other(who).astype(jnp.int32) for who in goals)
    pl.semaphore_wait(pltpu.get_barrier_semaphore(), 7 + away)

    def sems(send, recv, k):
        return send.at[k], recv.at[k]

    def block(k):
        return proj.at[k * 2 + c]

    def part(ref, begin, size):
        return ref.at[pl.ds(begin, size)]

    half_p, half_a = proj_ref.shape[0] // 2, att_own.shape[0] // 2
    begins = (0, half_p, half_p, 0)
    own_p = [
        push(
            part(proj_ref, begins[k], half_p), part(block(x), begins[k], half_p),
            sems(proj_send, proj_recv, k), (x_up, x_down)[k % 2],
        )
        for k in range(4)
    ]
    from_p = [
        push(
            part(proj_ref, begins[k], half_p),
            part(block((down_x, up_x)[k % 2]), begins[k], half_p),
            sems(proj_send, proj_recv, k), (x_up, x_down)[k % 2],
        )
        for k in range(4)
    ]

    def relay(ref, begin, size, pair_of, device):
        view = part(ref, begin, size)
        return push(view, view, pair_of, device)

    relay_p = [
        relay(block(down_x), 0, half_p, sems(proj_send, proj_recv, 4), x_up),
        relay(block(up_x), half_p, half_p, sems(proj_send, proj_recv, 5), x_down),
    ]
    far_p = [
        relay(block(far_x), 0, half_p, sems(proj_send, proj_recv, 4), x_up),
        relay(block(far_x), half_p, half_p, sems(proj_send, proj_recv, 5), x_down),
    ]
    own_across = push(proj_ref, block(x), sems(cross_send, cross_recv, 0), sibling)

    def across(k, slot):
        return push(block(k), block(k), sems(cross_send, cross_recv, slot), sibling)

    def from_sibling(k, slot):
        mine = proj.at[k * 2 + 1 - c]
        return push(mine, mine, sems(cross_send, cross_recv, slot), sibling)

    for copy in own_p:
        copy.start()
    own_across.start()

    loads[0].wait()
    attend(q_in_ref, latent_ref, lift, att_own)

    own_a = [
        push(att_own, att.at[y], sems(att_send, att_recv, 0), y_up),
        push(att_own, att.at[y], sems(att_send, att_recv, 1), y_down),
    ]
    from_a = [
        push(att_own, att.at[down_y], sems(att_send, att_recv, 0), y_up),
        push(att_own, att.at[up_y], sems(att_send, att_recv, 1), y_down),
    ]
    relay_a = [
        relay(att.at[down_y], 0, half_a, sems(att_send, att_recv, 2), y_up),
        relay(att.at[up_y], half_a, half_a, sems(att_send, att_recv, 3), y_down),
    ]
    far_a = [
        relay(att.at[far_y], 0, half_a, sems(att_send, att_recv, 2), y_up),
        relay(att.at[far_y], half_a, half_a, sems(att_send, att_recv, 3), y_down),
    ]
    for copy in own_a:
        copy.start()
    for k in range(2):
        from_p[k].wait_recv()
        relay_p[k].start()
    proj[pl.ds(x * 2 + c, 1)] = proj_ref[...][None]
    att[pl.ds(y, 1)] = att_own[...][None]
    route(ids_ref, num_ref, slot_ref, pick, comb)
    loads[1].wait()
    quantize_first, quantize_later = quantize_panel(
        us_ref, weight, u_ref, sel_ref, quant, wnat, cur, err, qi, lo, st, rs
    )
    quantize_first(0, 1)
    for k in range(2, 4):
        from_p[k].wait_recv()
    across(down_x, 1).start()
    across(up_x, 2).start()
    for copy in from_a:
        copy.wait_recv()
    for copy in relay_a:
        copy.start()
    quantize_first(1, 3)
    for copy in far_p:
        copy.wait_recv()
    across(far_x, 3).start()
    quantize_first(3, 4)
    for copy in far_a:
        copy.wait_recv()
    for slot, k in enumerate((x, down_x, up_x, far_x)):
        from_sibling(k, slot).wait_recv()

    tokens = att_own.shape[0]

    def partial(goal, half):
        left = proj[lax.div(goal, 2) * 2 + half]
        right = att[pl.ds(lax.rem(goal, 2) * 2, 2)].reshape(2 * tokens, -1)
        return lax.dot_general(
            left, right, (((1,), (1,)), ((), ())), preferred_element_type=F32
        )

    def rows(value, sub):
        return value[:, sub * tokens:(sub + 1) * tokens]

    my_slot = lax.rem(y, 2)

    def deliver(half, sub):
        who = goals[sub]
        return push(
            fin.at[sub, half], landed.at[my_slot, half],
            (fin_send.at[sub, half], fin_recv.at[my_slot, half]),
            (dp_of(x, who[0], c), who[1]),
        )

    def finish(half, sub, value):
        fin[sub, half] = value.astype(BF16)

        @pl.when(other(goals[sub]))
        def _():
            deliver(half, sub).start()

        @pl.when(jnp.logical_not(other(goals[sub])))
        def _():
            landed[pl.ds(my_slot, 1), half] = value.astype(BF16)[None]

    drain = ring_sum(
        z, at, ring, ring_send, ring_recv, partial, rows, finish, quantize_later
    )
    width = res_ref.shape[1]
    q_out = [
        pltpu.make_async_copy(
            quant.at[k], q_hbm.at[:, pl.ds(k * width, width)], load_sem.at[2 + k]
        )
        for k in range(NSUB)
    ]
    for copy in q_out:
        copy.start()
    drain()
    for slot, who in enumerate(sources):
        @pl.when(other(who))
        def _():
            for half in range(2):
                push(
                    fin.at[0, half], landed.at[slot, half],
                    (fin_send.at[0, half], fin_recv.at[slot, half]), sibling,
                ).wait_recv()

    total = landed[...].reshape(-1, tokens).astype(F32).T
    out_ref[...] = (res_ref[...].astype(F32) + total).astype(BF16)
    for copy in own_p + relay_p + own_a + relay_a + [own_across]:
        copy.wait_send()
    for slot, k in ((1, down_x), (2, up_x), (3, far_x)):
        across(k, slot).wait_send()
    for sub, who in enumerate(goals):
        @pl.when(other(who))
        def _():
            for side in range(2):
                deliver(side, sub).wait_send()
    for copy in q_out:
        copy.wait()


def back_kernel(
    res_ref, gain_ref, pick, comb, gate_hbm, up_hbm, q_hbm,
    moe_ref, gram_ref,
    weights, quant, outgoing, incoming, crossing, raw, scaled, square,
    ring_a, hidden, ring_b, rows_out, gathered, returning, returned,
    load_sem, out_send, out_recv, sib_send, sib_recv, sq_send, sq_recv,
    a_send, a_recv, b_send, b_recv, back_send, back_recv,
):
    x, y, c, z = place()
    at = lax.axis_index("dp")
    chip = x * SIDE + y
    sibling = (dp_of(x, y, 1 - c), z)

    def chip_at(k):
        return lax.rem(chip + k, CHIPS)

    def greet_chip(k, carry):
        greet((chip_at(k) * 2 + c, z))
        return carry

    def greet_z(k, carry):
        greet((at, lax.rem(z + k, RING)))
        return carry

    lax.fori_loop(1, CHIPS, greet_chip, 0)
    lax.fori_loop(1, RING, greet_z, 0)
    greet(sibling)
    width = res_ref.shape[1]
    loads = [
        pltpu.make_async_copy(gate_hbm, weights.at[0], load_sem.at[0]),
        pltpu.make_async_copy(up_hbm, weights.at[1], load_sem.at[1]),
    ] + [
        pltpu.make_async_copy(
            q_hbm.at[:, pl.ds(k * width, width)], quant.at[k], load_sem.at[2 + k]
        )
        for k in range(NSUB)
    ]
    for copy in loads:
        copy.start()
    unit = 2 * CAP
    count = CHIPS * unit
    half = count // 2
    r = lax.broadcasted_iota(jnp.int32, (count, count), 0)
    q = lax.broadcasted_iota(jnp.int32, (count, count), 1)
    spot = ((r >> 3) & 15) * unit + (((r >> 7) ^ c) & 1) * CAP + (r & 7)
    by_core = (q == spot).astype(F32).astype(BF16)
    spot_back = ((q >> 3) & 15) * unit + (((q >> 7) ^ c) & 1) * CAP + (q & 7)
    by_chip = (r == spot_back).astype(F32).astype(BF16)

    outgoing[...] = jnp.dot(pick[...], res_ref[...], preferred_element_type=F32).astype(BF16)
    pl.semaphore_wait(pltpu.get_barrier_semaphore(), CHIPS + RING - 1)

    def exchange(src, dst, send, recv, meanwhile):
        def rows_of(k):
            return pl.ds(pl.multiple_of(k * unit, unit), unit)

        def out(k):
            to = chip_at(k)
            return push(
                src.at[rows_of(to)], dst.at[rows_of(chip)], (send.at[k], recv.at[k]),
                (to * 2 + c, z),
            )

        def come(k):
            here = dst.at[rows_of(chip_at(CHIPS - k))]
            return push(here, here, (send.at[k], recv.at[k]), (chip_at(k) * 2 + c, z))

        def start(k, carry):
            out(k).start()
            return carry

        def arrive(k, carry):
            come(k).wait_recv()
            return carry

        def leave(k, carry):
            out(k).wait_send()
            return carry

        lax.fori_loop(1, CHIPS, start, 0)
        dst[rows_of(chip), :] = src[rows_of(chip), :]
        meanwhile()
        lax.fori_loop(1, CHIPS, arrive, 0)
        return leave

    leave_out = exchange(outgoing, incoming, out_send, out_recv, lambda: None)

    both = jnp.dot(by_core, incoming[...], preferred_element_type=F32).astype(BF16)
    raw[0:half, :] = both[:half]
    crossing[...] = both[half:]
    over = push(crossing, raw.at[pl.ds(half, half)], (sib_send.at[0], sib_recv.at[0]), sibling)
    over.start()
    over.wait_recv()

    wide = raw[...].astype(F32)
    square[pl.ds(z, 1)] = lax.dot_general(
        jnp.ones((8, wide.shape[1]), F32), wide * wide, (((1,), (1,)), ((), ())),
        preferred_element_type=F32, precision=lax.Precision.HIGHEST,
    )[None]

    def square_to(k):
        return push(
            square.at[z], square.at[z], (sq_send.at[k], sq_recv.at[k]),
            (at, lax.rem(z + k, RING)),
        )

    def square_from(k):
        here = square.at[lax.rem(z + RING - k, RING)]
        return push(here, here, (sq_send.at[k], sq_recv.at[k]), (at, lax.rem(z + k, RING)))

    def square_start(k, carry):
        square_to(k).start()
        return carry

    def square_arrive(k, carry):
        square_from(k).wait_recv()
        return carry

    def square_leave(k, carry):
        square_to(k).wait_send()
        return carry

    lax.fori_loop(1, RING, square_start, 0)
    scaled[...] = (wide * gain_ref[...].astype(F32)).astype(BF16)
    loads[0].wait()
    loads[1].wait()

    units = hidden.shape[1]
    sums = {}

    def partial_a(goal, side):
        return jnp.dot(
            scaled[...],
            weights[side, :, pl.ds(pl.multiple_of(goal * units, units), units)],
            preferred_element_type=F32,
        )

    def rows_a(value, sub):
        return value[sub * half:(sub + 1) * half]

    def finish_a(side, sub, value):
        sums[side, sub] = value

    drain_a = ring_sum(z, at, ring_a, a_send, a_recv, partial_a, rows_a, finish_a)

    lax.fori_loop(1, RING, square_arrive, 0)
    mean = jnp.sum(square[...], axis=0) / D
    scale = lax.rsqrt(mean + 1e-06).T[:, 0:1]
    gate = jnp.concatenate([sums[0, 0], sums[0, 1]], axis=0) * scale
    up = jnp.concatenate([sums[1, 0], sums[1, 1]], axis=0) * scale
    hidden[...] = (gate / (1.0 + jnp.exp(-gate)) * up).astype(BF16)
    gram_ref[...] = lax.dot_general(
        hidden[...], hidden[...], (((0,), (0,)), ((), ())), preferred_element_type=F32
    ) / count


    def partial_b(goal, side):
        return goal, side

    quarter = half // 2

    def rows_b(value, sub):
        goal, side = value
        begin = side * half + sub * quarter
        return jnp.dot(
            hidden[begin:begin + quarter, :], quant[goal], preferred_element_type=F32
        )

    def finish_b(side, sub, value):
        if side == 0:
            gathered[sub * quarter:(sub + 1) * quarter, :] = value.astype(BF16)
        else:
            rows_out[sub * quarter:(sub + 1) * quarter, :] = value.astype(BF16)

    for copy in loads[2:]:
        copy.wait()
    drain_b = ring_sum(z, at, ring_b, b_send, b_recv, partial_b, rows_b, finish_b)


    home = push(
        rows_out, gathered.at[pl.ds(half, half)], (sib_send.at[1], sib_recv.at[1]), sibling
    )
    home.start()
    home.wait_recv()
    returning[...] = jnp.dot(
        by_chip, gathered[...], preferred_element_type=F32
    ).astype(BF16)
    def settle():
        drain_a()
        drain_b()
        lax.fori_loop(1, CHIPS, leave_out, 0)
        lax.fori_loop(1, RING, square_leave, 0)

    leave_back = exchange(returning, returned, back_send, back_recv, settle)
    moe_ref[...] = lax.dot_general(
        comb[...], returned[...], (((0,), (0,)), ((), ())), preferred_element_type=F32
    ).astype(BF16)

    over.wait_send()
    home.wait_send()
    lax.fori_loop(1, CHIPS, leave_back, 0)
def front(us, projection, residual, queries, latent, ids, num, slots, weight, lift):
    width = weight.shape[1]
    tiles = width // (NSUB * LANES)
    vmem = pl.BlockSpec(memory_space=pltpu.VMEM)
    anywhere = pl.BlockSpec(memory_space=pl.ANY)
    dma = pltpu.SemaphoreType.DMA
    columns, depth = projection.shape
    tokens, block = residual.shape
    rows = 2 * CAP * CHIPS
    meet = (2, 2, 2, RING // 2)
    return pl.pallas_call(
        front_kernel,
        out_shape=(
            jax.ShapeDtypeStruct((tokens, block), BF16),
            jax.ShapeDtypeStruct((rows, tokens), BF16),
            jax.ShapeDtypeStruct((rows, tokens), BF16),
            jax.ShapeDtypeStruct((PANEL, width), BF16),
        ),
        in_specs=[pl.BlockSpec(memory_space=pltpu.SMEM)] + [vmem] * 9 + [anywhere] * 2,
        out_specs=(vmem, vmem, vmem, anywhere),
        scratch_shapes=[
            pltpu.VMEM((PANEL, width), BF16),
            pltpu.VMEM(lift.shape, BF16),
            pltpu.VMEM((NSUB, PANEL, width // NSUB), BF16),
            pltpu.VMEM((PANEL, width), F32),
            pltpu.VMEM((tiles, BLK * NSUB, LANES), F32),
            pltpu.VMEM((tiles, BLK * NSUB, LANES), F32),
            pltpu.VMEM((tiles, BLK * NSUB, LANES), F32),
            pltpu.VMEM((tiles, NSUB, LANES), F32),
            pltpu.VMEM((tiles, NSUB, LANES), F32),
            pltpu.VMEM((tiles, NSUB, LANES), F32),
            pltpu.VMEM((tokens, depth), BF16),
            pltpu.VMEM((2 * SIDE, columns, depth), BF16),
            pltpu.VMEM((SIDE, tokens, depth), BF16),
            pltpu.VMEM((2, 2, 2, RING // 2 + 1, columns, tokens), BF16),
            pltpu.VMEM((2, 2, columns, tokens), BF16),
            pltpu.VMEM((2, 2, columns, tokens), BF16),
            dma((2 + NSUB,)), dma((6,)), dma((6,)), dma((4,)), dma((4,)), dma((4,)), dma((4,)),
            dma(meet), dma(meet), dma((2, 2)), dma((2, 2)),
        ],
        compiler_params=pltpu.CompilerParams(
            vmem_limit_bytes=56 * 2**20, collective_id=0, has_side_effects=True
        ),
        name="front",
    )(
        us, us, jnp.asarray(selector(), BF16), projection, residual, queries, latent, ids, num,
        slots, weight, lift,
    )


def back(residual, gain, pick_any, combine, gate_w, up_w, quantized):
    vmem = pl.BlockSpec(memory_space=pltpu.VMEM)
    anywhere = pl.BlockSpec(memory_space=pl.ANY)
    dma = pltpu.SemaphoreType.DMA
    tokens, block = residual.shape
    rows = pick_any.shape[0]
    half = rows // 2
    wide = (rows, block)
    meet = (2, 2, 2, RING // 2)
    slots_of = (2, 2, 2, RING // 2 + 1)
    return pl.pallas_call(
        back_kernel,
        out_shape=(
            jax.ShapeDtypeStruct((tokens, block), BF16),
            jax.ShapeDtypeStruct((PANEL, PANEL), F32),
        ),
        in_specs=[vmem] * 4 + [anywhere] * 3,
        out_specs=(vmem, vmem),
        scratch_shapes=[
            pltpu.VMEM((2,) + gate_w.shape, BF16),
            pltpu.VMEM((NSUB, PANEL, block), BF16),
            pltpu.VMEM(wide, BF16),
            pltpu.VMEM(wide, BF16),
            pltpu.VMEM((half, block), BF16),
            pltpu.VMEM(wide, BF16),
            pltpu.VMEM(wide, BF16),
            pltpu.VMEM((RING, 8, rows), F32),
            pltpu.VMEM(slots_of + (half, PANEL), BF16),
            pltpu.VMEM((rows, PANEL), BF16),
            pltpu.VMEM(slots_of + (half // 2, block), BF16),
            pltpu.VMEM((half, block), BF16),
            pltpu.VMEM(wide, BF16),
            pltpu.VMEM(wide, BF16),
            pltpu.VMEM(wide, BF16),
            dma((2 + NSUB,)), dma((CHIPS,)), dma((CHIPS,)), dma((2,)), dma((2,)), dma((RING,)),
            dma((RING,)), dma(meet), dma(meet), dma(meet), dma(meet), dma((CHIPS,)),
            dma((CHIPS,)),
        ],
        compiler_params=pltpu.CompilerParams(
            vmem_limit_bytes=56 * 2**20, collective_id=1, has_side_effects=True
        ),
        name="back",
    )(residual, gain, pick_any, combine, gate_w, up_w, quantized)


def shards(
    residual_in,
    queries,
    latent,
    latent_up,
    out_proj,
    norm_gain,
    expert_ids,
    gate_num,
    slot_table,
    gate_proj,
    up_proj,
    down_proj,
    inv_chol,
):
    residual_out, pick_any, combine, quantized = front(
        inv_chol[0], out_proj.T, residual_in, queries.transpose(1, 2, 0), latent.T, expert_ids.T,
        gate_num.T, slot_table[None], down_proj[0], latent_up,
    )
    moe, gram = back(
        residual_out, norm_gain[None], pick_any, combine, gate_proj[0], up_proj[0], quantized
    )
    return residual_out, moe, quantized[None], gram[None]


def solution(mesh):
    placed = (
        P("dp", "tensor"),
        P("dp", "tensor", None),
        P("dp", None),
        P("tensor", None, None),
        P("tensor", "dp"),
        P("tensor"),
        P("dp", None),
        P("dp", None),
        P(),
        P("dp", "tensor", None),
        P("dp", "tensor", None),
        P("dp", "tensor", None),
        P("dp", "tensor", None),
    )
    return jax.shard_map(
        shards,
        mesh=mesh,
        in_specs=placed,
        out_specs=(
            P("dp", "tensor"),
            P("dp", "tensor"),
            P("dp", "tensor", None),
            P("dp", "tensor", None),
        ),
        check_vma=False,
    )
```

```python
import math

import jax
import jax.numpy as jnp
import numpy as np
from jax import lax
from jax.experimental import pallas as pl
from jax.experimental.pallas import tpu as pltpu
from jax.sharding import PartitionSpec as P

D = 7168
NOPE = 128
ROPE = 64
VHEAD = 128
LATENT = 512
PANEL = 128
BLK = 16
CAP = 8
NSUB = 8
LANES = 128
F32 = jnp.float32
BF16 = jnp.bfloat16


def _sin_coeffs():
    n = 400
    u = (0.5 * np.cos(np.pi * (np.arange(n) + 0.5) / (2 * n))) ** 2
    r = np.sqrt(u)
    target = np.sin(2 * np.pi * r) / (2 * np.pi * r)
    vand = np.vander(u, 8, increasing=True)
    return [float(c) for c in np.linalg.lstsq(vand * r[:, None], target * r, rcond=None)[0]]

SINC = _sin_coeffs()

def quantize_panel(us_ref, w_ref, u_ref, sel_ref, q_ref, wnat, cur, err, qi, lo, st, rs):
    tiles = w_ref.shape[1] // (NSUB * LANES)
    width = tiles * LANES

    def ranges():
        for c in range(NSUB):
            cols = slice(c * width, (c + 1) * width)
            chunk = w_ref[:, cols].astype(F32)
            wnat[:, cols] = chunk
            low = jnp.min(chunk, axis=0, keepdims=True)
            high = jnp.max(chunk, axis=0, keepdims=True)
            step = (high - low) / 15.0 + 1e-05
            inverse = 1.0 / step
            for j in range(tiles):
                lanes = slice(j * LANES, (j + 1) * LANES)
                lo[j, c:c + 1, :] = low[:, lanes]
                st[j, c:c + 1, :] = step[:, lanes]
                rs[j, c:c + 1, :] = inverse[:, lanes]

    def block(b, first):
        base = pl.multiple_of(b * BLK, BLK)
        for c in range(NSUB):
            for j in range(tiles):
                at = c * width + j * LANES
                cur[j, pl.ds(c, BLK, NSUB), :] = wnat[pl.ds(base, BLK), at:at + LANES]
        low, step, rstep = lo[...], st[...], rs[...]
        for i in range(BLK):
            rows = slice(i * NSUB, (i + 1) * NSUB)
            x = cur[:, rows, :]
            for k in range(i):
                x = x - us_ref[base + k, base + i] * err[:, k * NSUB:(k + 1) * NSUB, :]
            inv = 1.0 / jnp.full((NSUB, LANES), us_ref[base + i, base + i], F32)
            t = jnp.minimum(jnp.maximum((x - low) * rstep, 0.0), 15.0)
            r = t - jnp.floor(t + 0.5)
            v = r * r
            v2 = v * v
            poly = (SINC[0] + SINC[1] * v) + (SINC[2] + SINC[3] * v) * v2
            poly = poly + ((SINC[4] + SINC[5] * v) + (SINC[6] + SINC[7] * v) * v2) * (v2 * v2)
            level = low + step * (t - r * poly)
            err[:, rows, :] = (x - level) * inv[None]
            qi[:, rows, :] = level
        if first is not None:
            parts = jnp.concatenate(split3(u_ref[pl.ds(base, BLK), :]), axis=0)
            coupling = lax.dot_general(
                parts, sel_ref[...], (((0,), (0,)), ((), ())), preferred_element_type=F32
            ).astype(BF16)[first:, :]
        for c in range(NSUB):
            cols = slice(c * width, (c + 1) * width)
            spread = [qi[j, pl.ds(c, BLK, NSUB), :] for j in range(tiles)]
            q_ref[c, pl.ds(base, BLK), :] = jnp.concatenate(spread, axis=1).astype(BF16)
            if first is not None:
                spread = [err[j, pl.ds(c, BLK, NSUB), :] for j in range(tiles)]
                e = split3(jnp.concatenate(spread, axis=1))
                stacked = jnp.concatenate([e[p] for p in PART_E], axis=0)
                wnat[first:, cols] = wnat[first:, cols] - jnp.dot(
                    coupling, stacked, preferred_element_type=F32
                )

    def early(b, carry):
        block(b, BLK)
        return carry

    def first_half(begin, end):
        if begin == 0:
            ranges()
        lax.fori_loop(begin, end, early, 0)

    def later(step):
        if isinstance(step, int) and step == 3:
            block(7, None)
        else:
            block(4 + step, 5 * BLK)

    return first_half, later


PART_U = (0, 0, 0, 1, 1, 2, 1, 2)
PART_E = (0, 1, 2, 0, 1, 0, 2, 1)

def split3(a):
    a1 = a.astype(BF16)
    rest = a - a1.astype(F32)
    a2 = rest.astype(BF16)
    return a1, a2, (rest - a2.astype(F32)).astype(BF16)


def selector():
    sel = np.zeros((3 * BLK, 8 * BLK), np.float32)
    for slot, part in enumerate(PART_U):
        for i in range(BLK):
            sel[part * BLK + i, slot * BLK + i] = 1
    return sel


MESH = pl.DeviceIdType.MESH
SIDE = 4
RING = 8
CHIPS = SIDE * SIDE


def place():
    at = lax.axis_index("dp")
    x = lax.div(at, 2 * SIDE)
    y = lax.rem(lax.div(at, 2), SIDE)
    return x, y, lax.rem(at, 2), lax.axis_index("tensor")


def dp_of(x, y, c):
    return (x * SIDE + y) * 2 + c


def push(src, dst, sems, device):
    return pltpu.make_async_remote_copy(
        src_ref=src, dst_ref=dst, send_sem=sems[0], recv_sem=sems[1], device_id=device,
        device_id_type=MESH,
    )


def greet(device):
    pl.semaphore_signal(
        pltpu.get_barrier_semaphore(), inc=1, device_id=device, device_id_type=MESH
    )


def ring_sum(z, at, ring, send, recv, partial, rows, finish, meanwhile=lambda step: None):
    def length(side, half):
        return RING // 2 if side == half else RING // 2 - 1

    def hop(side, half, sub, slot):
        to = lax.rem(z + (1 if side == 0 else RING - 1), RING)
        return push(
            ring.at[side, half, sub, slot],
            ring.at[side, half, sub, slot + 1],
            (send.at[side, half, sub, slot], recv.at[side, half, sub, slot]),
            (at, to),
        )

    def goal(side, half, step):
        away = length(side, half) - step
        return lax.rem(z + (away if side == 0 else RING - away), RING)

    streams = [(0, 0), (1, 1), (0, 1), (1, 0)]
    for side, half in streams:
        own = partial(goal(side, half, 0), half)
        for sub in range(2):
            ring[side, half, sub, 0] = rows(own, sub).astype(BF16)
            hop(side, half, sub, 0).start()
    meanwhile(0)

    def advance(step, members):
        for side, half in members:
            own = partial(goal(side, half, step), half)
            for sub in range(2):
                hop(side, half, sub, step - 1).wait_recv()
                value = rows(own, sub) + ring[side, half, sub, step].astype(F32)
                ring[side, half, sub, step] = value.astype(BF16)
                hop(side, half, sub, step).start()
        meanwhile(step)

    def middle(step, carry):
        advance(step, streams)
        return carry

    lax.fori_loop(1, RING // 2 - 1, middle, 0)
    advance(RING // 2 - 1, streams[:2])
    for half in (1, 0):
        own = partial(z, half)
        for sub in range(2):
            value = rows(own, sub)
            for side in (1 - half, half):
                last = length(side, half)
                hop(side, half, sub, last - 1).wait_recv()
                value = value + ring[side, half, sub, last].astype(F32)
            finish(half, sub, value)

    def drain():
        def left(step, members):
            for side, half in members:
                for sub in range(2):
                    hop(side, half, sub, step).wait_send()

        def sent(step, carry):
            left(step, streams)
            return carry

        lax.fori_loop(0, RING // 2 - 1, sent, 0)
        left(RING // 2 - 1, streams[:2])

    return drain


def attend(q_ref, latent_ref, up, att_ref):
    heads, tokens = q_ref.shape[0], q_ref.shape[2]
    rows = (((0,), (0,)), ((), ()))
    low = latent_ref[:LATENT, :]
    rotary = latent_ref[LATENT:, :]
    causal = lax.broadcasted_iota(jnp.int32, (tokens, tokens), 1) <= lax.broadcasted_iota(
        jnp.int32, (tokens, tokens), 0
    )
    for h in range(heads):
        both = lax.dot_general(up[h], low, rows, preferred_element_type=F32).astype(BF16)
        key = jnp.concatenate([both[:NOPE], rotary], axis=0)
        scores = lax.dot_general(q_ref[h], key, rows, preferred_element_type=F32) * (
            1.0 / math.sqrt(NOPE + ROPE)
        )
        scores = jnp.where(causal, scores, -1e30)
        expo = jnp.exp(scores - jnp.max(scores, axis=1, keepdims=True))
        probs = (expo / jnp.sum(expo, axis=1, keepdims=True)).astype(BF16)
        att_ref[:, h * VHEAD:(h + 1) * VHEAD] = lax.dot_general(
            probs, both[NOPE:], (((1,), (1,)), ((), ())), preferred_element_type=F32
        ).astype(BF16)


def route(ids_ref, num_ref, slot_ref, pick_ref, comb_ref):
    tokens, experts_all = ids_ref.shape[1], slot_ref.shape[1]
    slots = pick_ref.shape[0] // CAP
    names = lax.broadcasted_iota(jnp.int32, (experts_all, tokens), 0)
    picks = jnp.zeros((experts_all, tokens), F32)
    gates = jnp.zeros((experts_all, tokens), F32)
    for k in range(ids_ref.shape[0]):
        hit = ids_ref[k:k + 1, :] == names
        picks = jnp.where(hit, 1.0, picks)
        gates = jnp.where(hit, num_ref[k:k + 1, :].astype(F32), gates)
    kept = jnp.where(
        slot_ref[...] == lax.broadcasted_iota(jnp.int32, (slots, experts_all), 0), 1.0, 0.0
    ).astype(BF16)
    slot_picks = jnp.dot(kept, picks.astype(BF16), preferred_element_type=F32)
    slot_gates = jnp.dot(kept, gates.astype(BF16), preferred_element_type=F32)
    earlier = jnp.where(
        lax.broadcasted_iota(jnp.int32, (tokens, tokens), 0)
        < lax.broadcasted_iota(jnp.int32, (tokens, tokens), 1), 1.0, 0.0
    ).astype(BF16)
    before = jnp.dot(slot_picks.astype(BF16), earlier, preferred_element_type=F32)
    before = jnp.where(slot_picks > 0.5, before, -1.0)
    shape = (slots, CAP, tokens)
    spot = lax.broadcasted_iota(jnp.int32, shape, 1).astype(F32)
    lands = jnp.broadcast_to(before[:, None, :], shape) == spot
    weight = jnp.broadcast_to(slot_gates[:, None, :], shape) / 256.0
    pick_ref[...] = jnp.where(lands, 1.0, 0.0).reshape(slots * CAP, tokens).astype(BF16)
    comb_ref[...] = jnp.where(lands, weight, 0.0).reshape(slots * CAP, tokens).astype(BF16)


def front_kernel(
    us_ref, u_ref, sel_ref, proj_ref, res_ref, q_in_ref, latent_ref, ids_ref, num_ref, slot_ref,
    w_hbm, lift_hbm,
    out_ref, pick, comb, q_hbm,
    weight, lift, quant, wnat, cur, err, qi, lo, st, rs,
    att_own, proj, att, ring, fin, landed,
    load_sem, proj_send, proj_recv, cross_send, cross_recv, att_send, att_recv,
    ring_send, ring_recv, fin_send, fin_recv,
):
    x, y, c, z = place()
    at = lax.axis_index("dp")
    up_x, down_x = lax.rem(x + 1, SIDE), lax.rem(x + SIDE - 1, SIDE)
    up_y, down_y = lax.rem(y + 1, SIDE), lax.rem(y + SIDE - 1, SIDE)
    far_x, far_y = lax.rem(x + 2, SIDE), lax.rem(y + 2, SIDE)
    x_up, x_down = (dp_of(up_x, y, c), z), (dp_of(down_x, y, c), z)
    y_up, y_down = (dp_of(x, up_y, c), z), (dp_of(x, down_y, c), z)
    sibling = (dp_of(x, y, 1 - c), z)
    pair = lax.div(z, 2) * 2
    bit = lax.rem(z, 2)
    goal_z = pair + lax.div(y, 2)
    goals = [(2 * bit + sub, goal_z) for sub in range(2)]
    sources = [(2 * bit + slot, goal_z) for slot in range(2)]

    def other(who):
        return jnp.logical_not(jnp.logical_and(who[0] == y, who[1] == z))

    for device in (
        x_up, x_down, y_up, y_down, sibling,
        (at, lax.rem(z + 1, RING)), (at, lax.rem(z + RING - 1, RING)),
    ):
        greet(device)
    for who in sources:
        @pl.when(other(who))
        def _():
            greet((dp_of(x, who[0], c), who[1]))
    loads = [
        pltpu.make_async_copy(lift_hbm, lift, load_sem.at[0]),
        pltpu.make_async_copy(w_hbm, weight, load_sem.at[1]),
    ]
    for copy in loads:
        copy.start()
    away = sum(other(who).astype(jnp.int32) for who in goals)
    pl.semaphore_wait(pltpu.get_barrier_semaphore(), 7 + away)

    def sems(send, recv, k):
        return send.at[k], recv.at[k]

    def block(k):
        return proj.at[k * 2 + c]

    def part(ref, begin, size):
        return ref.at[pl.ds(begin, size)]

    half_p, half_a = proj_ref.shape[0] // 2, att_own.shape[0] // 2
    begins = (0, half_p, half_p, 0)
    own_p = [
        push(
            part(proj_ref, begins[k], half_p), part(block(x), begins[k], half_p),
            sems(proj_send, proj_recv, k), (x_up, x_down)[k % 2],
        )
        for k in range(4)
    ]
    from_p = [
        push(
            part(proj_ref, begins[k], half_p),
            part(block((down_x, up_x)[k % 2]), begins[k], half_p),
            sems(proj_send, proj_recv, k), (x_up, x_down)[k % 2],
        )
        for k in range(4)
    ]

    def relay(ref, begin, size, pair_of, device):
        view = part(ref, begin, size)
        return push(view, view, pair_of, device)

    relay_p = [
        relay(block(down_x), 0, half_p, sems(proj_send, proj_recv, 4), x_up),
        relay(block(up_x), half_p, half_p, sems(proj_send, proj_recv, 5), x_down),
    ]
    far_p = [
        relay(block(far_x), 0, half_p, sems(proj_send, proj_recv, 4), x_up),
        relay(block(far_x), half_p, half_p, sems(proj_send, proj_recv, 5), x_down),
    ]
    own_across = push(proj_ref, block(x), sems(cross_send, cross_recv, 0), sibling)

    def across(k, slot):
        return push(block(k), block(k), sems(cross_send, cross_recv, slot), sibling)

    def from_sibling(k, slot):
        mine = proj.at[k * 2 + 1 - c]
        return push(mine, mine, sems(cross_send, cross_recv, slot), sibling)

    for copy in own_p:
        copy.start()
    own_across.start()

    loads[0].wait()
    attend(q_in_ref, latent_ref, lift, att_own)

    own_a = [
        push(att_own, att.at[y], sems(att_send, att_recv, 0), y_up),
        push(att_own, att.at[y], sems(att_send, att_recv, 1), y_down),
    ]
    from_a = [
        push(att_own, att.at[down_y], sems(att_send, att_recv, 0), y_up),
        push(att_own, att.at[up_y], sems(att_send, att_recv, 1), y_down),
    ]
    relay_a = [
        relay(att.at[down_y], 0, half_a, sems(att_send, att_recv, 2), y_up),
        relay(att.at[up_y], half_a, half_a, sems(att_send, att_recv, 3), y_down),
    ]
    far_a = [
        relay(att.at[far_y], 0, half_a, sems(att_send, att_recv, 2), y_up),
        relay(att.at[far_y], half_a, half_a, sems(att_send, att_recv, 3), y_down),
    ]
    for copy in own_a:
        copy.start()
    for k in range(2):
        from_p[k].wait_recv()
        relay_p[k].start()
    proj[pl.ds(x * 2 + c, 1)] = proj_ref[...][None]
    att[pl.ds(y, 1)] = att_own[...][None]
    route(ids_ref, num_ref, slot_ref, pick, comb)
    loads[1].wait()
    quantize_first, quantize_later = quantize_panel(
        us_ref, weight, u_ref, sel_ref, quant, wnat, cur, err, qi, lo, st, rs
    )
    quantize_first(0, 1)
    for k in range(2, 4):
        from_p[k].wait_recv()
    across(down_x, 1).start()
    across(up_x, 2).start()
    for copy in from_a:
        copy.wait_recv()
    for copy in relay_a:
        copy.start()
    quantize_first(1, 3)
    for copy in far_p:
        copy.wait_recv()
    across(far_x, 3).start()
    quantize_first(3, 4)
    for copy in far_a:
        copy.wait_recv()
    for slot, k in enumerate((x, down_x, up_x, far_x)):
        from_sibling(k, slot).wait_recv()

    tokens = att_own.shape[0]

    def partial(goal, half):
        left = proj[lax.div(goal, 2) * 2 + half]
        right = att[pl.ds(lax.rem(goal, 2) * 2, 2)].reshape(2 * tokens, -1)
        return lax.dot_general(
            left, right, (((1,), (1,)), ((), ())), preferred_element_type=F32
        )

    def rows(value, sub):
        return value[:, sub * tokens:(sub + 1) * tokens]

    my_slot = lax.rem(y, 2)

    def deliver(half, sub):
        who = goals[sub]
        return push(
            fin.at[sub, half], landed.at[my_slot, half],
            (fin_send.at[sub, half], fin_recv.at[my_slot, half]),
            (dp_of(x, who[0], c), who[1]),
        )

    def finish(half, sub, value):
        fin[sub, half] = value.astype(BF16)

        @pl.when(other(goals[sub]))
        def _():
            deliver(half, sub).start()

        @pl.when(jnp.logical_not(other(goals[sub])))
        def _():
            landed[pl.ds(my_slot, 1), half] = value.astype(BF16)[None]

    drain = ring_sum(
        z, at, ring, ring_send, ring_recv, partial, rows, finish, quantize_later
    )
    width = res_ref.shape[1]
    q_out = [
        pltpu.make_async_copy(
            quant.at[k], q_hbm.at[:, pl.ds(k * width, width)], load_sem.at[2 + k]
        )
        for k in range(NSUB)
    ]
    for copy in q_out:
        copy.start()
    drain()
    for slot, who in enumerate(sources):
        @pl.when(other(who))
        def _():
            for half in range(2):
                push(
                    fin.at[0, half], landed.at[slot, half],
                    (fin_send.at[0, half], fin_recv.at[slot, half]), sibling,
                ).wait_recv()

    total = landed[...].reshape(-1, tokens).astype(F32).T
    out_ref[...] = (res_ref[...].astype(F32) + total).astype(BF16)
    for copy in own_p + relay_p + own_a + relay_a + [own_across]:
        copy.wait_send()
    for slot, k in ((1, down_x), (2, up_x), (3, far_x)):
        across(k, slot).wait_send()
    for sub, who in enumerate(goals):
        @pl.when(other(who))
        def _():
            for side in range(2):
                deliver(side, sub).wait_send()
    for copy in q_out:
        copy.wait()


def back_kernel(
    res_ref, gain_ref, pick, comb, gate_hbm, up_hbm, q_hbm,
    moe_ref, gram_ref,
    weights, quant, outgoing, incoming, crossing, raw, scaled, square,
    ring_a, hidden, ring_b, rows_out, gathered, returning, returned,
    load_sem, out_send, out_recv, sib_send, sib_recv, sq_send, sq_recv,
    a_send, a_recv, b_send, b_recv, back_send, back_recv,
):
    x, y, c, z = place()
    at = lax.axis_index("dp")
    chip = x * SIDE + y
    sibling = (dp_of(x, y, 1 - c), z)

    def chip_at(k):
        return lax.rem(chip + k, CHIPS)

    def greet_chip(k, carry):
        greet((chip_at(k) * 2 + c, z))
        return carry

    def greet_z(k, carry):
        greet((at, lax.rem(z + k, RING)))
        return carry

    lax.fori_loop(1, CHIPS, greet_chip, 0)
    lax.fori_loop(1, RING, greet_z, 0)
    greet(sibling)
    width = res_ref.shape[1]
    loads = [
        pltpu.make_async_copy(gate_hbm, weights.at[0], load_sem.at[0]),
        pltpu.make_async_copy(up_hbm, weights.at[1], load_sem.at[1]),
    ] + [
        pltpu.make_async_copy(
            q_hbm.at[:, pl.ds(k * width, width)], quant.at[k], load_sem.at[2 + k]
        )
        for k in range(NSUB)
    ]
    for copy in loads:
        copy.start()
    unit = 2 * CAP
    count = CHIPS * unit
    half = count // 2
    r = lax.broadcasted_iota(jnp.int32, (count, count), 0)
    q = lax.broadcasted_iota(jnp.int32, (count, count), 1)
    spot = ((r >> 3) & 15) * unit + (((r >> 7) ^ c) & 1) * CAP + (r & 7)
    by_core = (q == spot).astype(F32).astype(BF16)
    spot_back = ((q >> 3) & 15) * unit + (((q >> 7) ^ c) & 1) * CAP + (q & 7)
    by_chip = (r == spot_back).astype(F32).astype(BF16)

    outgoing[...] = jnp.dot(pick[...], res_ref[...], preferred_element_type=F32).astype(BF16)
    pl.semaphore_wait(pltpu.get_barrier_semaphore(), CHIPS + RING - 1)

    def exchange(src, dst, send, recv, meanwhile):
        def rows_of(k):
            return pl.ds(pl.multiple_of(k * unit, unit), unit)

        def out(k):
            to = chip_at(k)
            return push(
                src.at[rows_of(to)], dst.at[rows_of(chip)], (send.at[k], recv.at[k]),
                (to * 2 + c, z),
            )

        def come(k):
            here = dst.at[rows_of(chip_at(CHIPS - k))]
            return push(here, here, (send.at[k], recv.at[k]), (chip_at(k) * 2 + c, z))

        def start(k, carry):
            out(k).start()
            return carry

        def arrive(k, carry):
            come(k).wait_recv()
            return carry

        def leave(k, carry):
            out(k).wait_send()
            return carry

        lax.fori_loop(1, CHIPS, start, 0)
        dst[rows_of(chip), :] = src[rows_of(chip), :]
        meanwhile()
        lax.fori_loop(1, CHIPS, arrive, 0)
        return leave

    leave_out = exchange(outgoing, incoming, out_send, out_recv, lambda: None)

    crossing[...] = jnp.dot(
        by_core[half:], incoming[...], preferred_element_type=F32
    ).astype(BF16)
    over = push(crossing, raw.at[pl.ds(half, half)], (sib_send.at[0], sib_recv.at[0]), sibling)
    over.start()
    raw[0:half, :] = jnp.dot(
        by_core[:half], incoming[...], preferred_element_type=F32
    ).astype(BF16)
    over.wait_recv()

    wide = raw[...].astype(F32)
    square[pl.ds(z, 1)] = lax.dot_general(
        jnp.ones((8, wide.shape[1]), F32), wide * wide, (((1,), (1,)), ((), ())),
        preferred_element_type=F32, precision=lax.Precision.HIGHEST,
    )[None]

    def square_to(k):
        return push(
            square.at[z], square.at[z], (sq_send.at[k], sq_recv.at[k]),
            (at, lax.rem(z + k, RING)),
        )

    def square_from(k):
        here = square.at[lax.rem(z + RING - k, RING)]
        return push(here, here, (sq_send.at[k], sq_recv.at[k]), (at, lax.rem(z + k, RING)))

    def square_start(k, carry):
        square_to(k).start()
        return carry

    def square_arrive(k, carry):
        square_from(k).wait_recv()
        return carry

    def square_leave(k, carry):
        square_to(k).wait_send()
        return carry

    lax.fori_loop(1, RING, square_start, 0)
    scaled[...] = (wide * gain_ref[...].astype(F32)).astype(BF16)
    loads[0].wait()
    loads[1].wait()

    units = hidden.shape[1]
    sums = {}

    def partial_a(goal, side):
        return jnp.dot(
            scaled[...],
            weights[side, :, pl.ds(pl.multiple_of(goal * units, units), units)],
            preferred_element_type=F32,
        )

    def rows_a(value, sub):
        return value[sub * half:(sub + 1) * half]

    def finish_a(side, sub, value):
        sums[side, sub] = value

    drain_a = ring_sum(z, at, ring_a, a_send, a_recv, partial_a, rows_a, finish_a)

    lax.fori_loop(1, RING, square_arrive, 0)
    mean = jnp.sum(square[...], axis=0) / D
    scale = lax.rsqrt(mean + 1e-06).T[:, 0:1]
    gate = jnp.concatenate([sums[0, 0], sums[0, 1]], axis=0) * scale
    up = jnp.concatenate([sums[1, 0], sums[1, 1]], axis=0) * scale
    hidden[...] = (gate / (1.0 + jnp.exp(-gate)) * up).astype(BF16)


    def partial_b(goal, side):
        return goal, side

    quarter = half // 2

    def rows_b(value, sub):
        goal, side = value
        begin = side * half + sub * quarter
        return jnp.dot(
            hidden[begin:begin + quarter, :], quant[goal], preferred_element_type=F32
        )

    def home(sub):
        return push(
            rows_out.at[pl.ds(sub * quarter, quarter)],
            gathered.at[pl.ds(half + sub * quarter, quarter)],
            (sib_send.at[1 + sub], sib_recv.at[1 + sub]), sibling,
        )

    def finish_b(side, sub, value):
        if side == 0:
            gathered[sub * quarter:(sub + 1) * quarter, :] = value.astype(BF16)
        else:
            rows_out[sub * quarter:(sub + 1) * quarter, :] = value.astype(BF16)
            home(sub).start()

    for copy in loads[2:]:
        copy.wait()
    drain_b = ring_sum(z, at, ring_b, b_send, b_recv, partial_b, rows_b, finish_b)


    for sub in range(2):
        home(sub).wait_recv()
    returning[...] = jnp.dot(
        by_chip, gathered[...], preferred_element_type=F32
    ).astype(BF16)
    def settle():
        gram_ref[...] = lax.dot_general(
            hidden[...], hidden[...], (((0,), (0,)), ((), ())), preferred_element_type=F32
        ) / count
        drain_a()
        drain_b()
        lax.fori_loop(1, CHIPS, leave_out, 0)
        lax.fori_loop(1, RING, square_leave, 0)

    leave_back = exchange(returning, returned, back_send, back_recv, settle)
    moe_ref[...] = lax.dot_general(
        comb[...], returned[...], (((0,), (0,)), ((), ())), preferred_element_type=F32
    ).astype(BF16)

    over.wait_send()
    for sub in range(2):
        home(sub).wait_send()
    lax.fori_loop(1, CHIPS, leave_back, 0)
def front(us, projection, residual, queries, latent, ids, num, slots, weight, lift):
    width = weight.shape[1]
    tiles = width // (NSUB * LANES)
    vmem = pl.BlockSpec(memory_space=pltpu.VMEM)
    anywhere = pl.BlockSpec(memory_space=pl.ANY)
    dma = pltpu.SemaphoreType.DMA
    columns, depth = projection.shape
    tokens, block = residual.shape
    rows = 2 * CAP * CHIPS
    meet = (2, 2, 2, RING // 2)
    return pl.pallas_call(
        front_kernel,
        out_shape=(
            jax.ShapeDtypeStruct((tokens, block), BF16),
            jax.ShapeDtypeStruct((rows, tokens), BF16),
            jax.ShapeDtypeStruct((rows, tokens), BF16),
            jax.ShapeDtypeStruct((PANEL, width), BF16),
        ),
        in_specs=[pl.BlockSpec(memory_space=pltpu.SMEM)] + [vmem] * 9 + [anywhere] * 2,
        out_specs=(vmem, vmem, vmem, anywhere),
        scratch_shapes=[
            pltpu.VMEM((PANEL, width), BF16),
            pltpu.VMEM(lift.shape, BF16),
            pltpu.VMEM((NSUB, PANEL, width // NSUB), BF16),
            pltpu.VMEM((PANEL, width), F32),
            pltpu.VMEM((tiles, BLK * NSUB, LANES), F32),
            pltpu.VMEM((tiles, BLK * NSUB, LANES), F32),
            pltpu.VMEM((tiles, BLK * NSUB, LANES), F32),
            pltpu.VMEM((tiles, NSUB, LANES), F32),
            pltpu.VMEM((tiles, NSUB, LANES), F32),
            pltpu.VMEM((tiles, NSUB, LANES), F32),
            pltpu.VMEM((tokens, depth), BF16),
            pltpu.VMEM((2 * SIDE, columns, depth), BF16),
            pltpu.VMEM((SIDE, tokens, depth), BF16),
            pltpu.VMEM((2, 2, 2, RING // 2 + 1, columns, tokens), BF16),
            pltpu.VMEM((2, 2, columns, tokens), BF16),
            pltpu.VMEM((2, 2, columns, tokens), BF16),
            dma((2 + NSUB,)), dma((6,)), dma((6,)), dma((4,)), dma((4,)), dma((4,)), dma((4,)),
            dma(meet), dma(meet), dma((2, 2)), dma((2, 2)),
        ],
        compiler_params=pltpu.CompilerParams(
            vmem_limit_bytes=56 * 2**20, collective_id=0, has_side_effects=True
        ),
        name="front",
    )(
        us, us, jnp.asarray(selector(), BF16), projection, residual, queries, latent, ids, num,
        slots, weight, lift,
    )


def back(residual, gain, pick_any, combine, gate_w, up_w, quantized):
    vmem = pl.BlockSpec(memory_space=pltpu.VMEM)
    anywhere = pl.BlockSpec(memory_space=pl.ANY)
    dma = pltpu.SemaphoreType.DMA
    tokens, block = residual.shape
    rows = pick_any.shape[0]
    half = rows // 2
    wide = (rows, block)
    meet = (2, 2, 2, RING // 2)
    slots_of = (2, 2, 2, RING // 2 + 1)
    return pl.pallas_call(
        back_kernel,
        out_shape=(
            jax.ShapeDtypeStruct((tokens, block), BF16),
            jax.ShapeDtypeStruct((PANEL, PANEL), F32),
        ),
        in_specs=[vmem] * 4 + [anywhere] * 3,
        out_specs=(vmem, vmem),
        scratch_shapes=[
            pltpu.VMEM((2,) + gate_w.shape, BF16),
            pltpu.VMEM((NSUB, PANEL, block), BF16),
            pltpu.VMEM(wide, BF16),
            pltpu.VMEM(wide, BF16),
            pltpu.VMEM((half, block), BF16),
            pltpu.VMEM(wide, BF16),
            pltpu.VMEM(wide, BF16),
            pltpu.VMEM((RING, 8, rows), F32),
            pltpu.VMEM(slots_of + (half, PANEL), BF16),
            pltpu.VMEM((rows, PANEL), BF16),
            pltpu.VMEM(slots_of + (half // 2, block), BF16),
            pltpu.VMEM((half, block), BF16),
            pltpu.VMEM(wide, BF16),
            pltpu.VMEM(wide, BF16),
            pltpu.VMEM(wide, BF16),
            dma((2 + NSUB,)), dma((CHIPS,)), dma((CHIPS,)), dma((3,)), dma((3,)), dma((RING,)),
            dma((RING,)), dma(meet), dma(meet), dma(meet), dma(meet), dma((CHIPS,)),
            dma((CHIPS,)),
        ],
        compiler_params=pltpu.CompilerParams(
            vmem_limit_bytes=56 * 2**20, collective_id=1, has_side_effects=True
        ),
        name="back",
    )(residual, gain, pick_any, combine, gate_w, up_w, quantized)


def shards(
    residual_in,
    queries,
    latent,
    latent_up,
    out_proj,
    norm_gain,
    expert_ids,
    gate_num,
    slot_table,
    gate_proj,
    up_proj,
    down_proj,
    inv_chol,
):
    residual_out, pick_any, combine, quantized = front(
        inv_chol[0], out_proj.T, residual_in, queries.transpose(1, 2, 0), latent.T, expert_ids.T,
        gate_num.T, slot_table[None], down_proj[0], latent_up,
    )
    moe, gram = back(
        residual_out, norm_gain[None], pick_any, combine, gate_proj[0], up_proj[0], quantized
    )
    return residual_out, moe, quantized[None], gram[None]


def solution(mesh):
    placed = (
        P("dp", "tensor"),
        P("dp", "tensor", None),
        P("dp", None),
        P("tensor", None, None),
        P("tensor", "dp"),
        P("tensor"),
        P("dp", None),
        P("dp", None),
        P(),
        P("dp", "tensor", None),
        P("dp", "tensor", None),
        P("dp", "tensor", None),
        P("dp", "tensor", None),
    )
    return jax.shard_map(
        shards,
        mesh=mesh,
        in_specs=placed,
        out_specs=(
            P("dp", "tensor"),
            P("dp", "tensor"),
            P("dp", "tensor", None),
            P("dp", "tensor", None),
        ),
        check_vma=False,
    )
```
